256 devices in a mesh: seq: 64 (over x, z, core), chan: 4 (over y).
Axes of the slice: x: 4, y: 4, z: 8, core: 2. Of those that a mesh axis runs over, the one named last changes fastest.
Arguments:
- query_proj: bfloat16 [16384, 4096], P('seq', 'chan'), may hold values from -6 to 6
- key_proj: bfloat16 [16384, 4096], P('seq', 'chan'), may hold values from -6 to 6
- value_proj: bfloat16 [16384, 4096], P('seq', 'chan'), may hold values from -6 to 6
- residues: float32 [4096, 16], P('chan'), may hold values from -0.09375 to 0.09375
- pole_rates: float32 [4096, 16], P('chan'), may hold values from 0.5 to 1000
- skip_gain: float32 [4096], P('chan'), may hold values from 0.25 to 1
- norm_gain: float32 [4096], P('chan'), may hold values from 0.1 to 1.9
Outputs:
- normed: bfloat16 [16384, 4096], P('seq', 'chan')
The draws below stay inside these ranges and needn't reach their ends.
All inputs are finite; a program needn't handle non-finite values.
Results may differ from the reference program's by a relative error of at most 0.001.
Values sent between devices are 32-bit elements; how exact they have to be, the bound alone decides.
A program may use at most 128 MiB of HBM per device.

```python
import math
import jax
import jax.numpy as jnp
from jax import lax

D = 4096
M = 16
TOK_DEV = 256
TOKENS = 16384


def steps_of(key, shape, shards, smallest, largest):
    loudness = 1.0
    for position, blocks in shards:
        steps = jax.random.uniform(jax.random.fold_in(jax.random.fold_in(key, 6), position), (blocks,), jnp.float32, smallest / len(shards), largest / len(shards))
        loudness = loudness * jnp.repeat(jnp.exp(steps), shape[position] // blocks).reshape((-1,) + (1,) * (len(shape) - 1 - position))
    return loudness


def noise(own_key, dims, width, reach, shards=(), held_as=jnp.bfloat16):
    drawn = width * jax.random.normal(own_key, dims, jnp.float32)
    if shards:
        drawn = drawn * steps_of(own_key, dims, shards, -0.22, 0.18)
    return jnp.clip(drawn, -reach, reach).astype(held_as)


def setup_inputs(seed: int = 0) -> dict:
    seeds = jax.random.split(jax.random.key(seed), 8)
    query_proj = noise(seeds[0], (TOKENS, D), 1.0, 6.0, ((0, 64), (1, 4)))
    key_proj = noise(seeds[1], (TOKENS, D), 1.0, 6.0, ((0, 64), (1, 4)))
    value_proj = noise(seeds[2], (TOKENS, D), 1.0, 6.0, ((0, 64), (1, 4)))
    residues = noise(seeds[3], (D, M), (M * TOK_DEV) ** -0.5, 0.09375, ((0, 4),), jnp.float32)
    pole_rates = jnp.clip(jnp.exp(math.log(1000.0) - 7.6009025 * jax.random.uniform(seeds[4], (D, M), jnp.float32) ** steps_of(seeds[4], (D, M), ((0, 4),), -0.2, 0.2)), 0.5, 1000.0)
    skip_gain = jnp.clip(0.25 + 0.75 * jax.random.uniform(seeds[5], (D,), jnp.float32) ** steps_of(seeds[5], (D,), ((0, 4),), -0.2, 0.2), 0.25, 1.0)
    norm_gain = jnp.clip(1.0 + 0.18 * jax.random.normal(seeds[6], (D,), jnp.float32), 0.1, 1.9)
    return {"query_proj": query_proj, "key_proj": key_proj, "value_proj": value_proj, "residues": residues, "pole_rates": pole_rates, "skip_gain": skip_gain, "norm_gain": norm_gain}


def filter_block(pieces):
    gated_rows, residue_block, rate_block = pieces
    length = gated_rows.shape[0]
    positions = jnp.arange(length, dtype=jnp.float32)
    decays = jnp.exp(-rate_block[None, :, :] * positions[:, None, None] / length)
    kernel = lax.optimization_barrier(jnp.sum(residue_block[None, :, :] * decays, axis=2))
    spectrum = jnp.fft.rfft(gated_rows, n=2 * length, axis=0) * jnp.fft.rfft(kernel, n=2 * length, axis=0)
    return jnp.fft.irfft(spectrum, n=2 * length, axis=0)[:length].astype(gated_rows.dtype)

def reference(query_proj, key_proj, value_proj, residues, pole_rates, skip_gain, norm_gain):
    gated = key_proj.astype(jnp.float32) * value_proj.astype(jnp.float32)
    block_width = math.gcd(D, 128)
    nblocks = D // block_width
    pieces = (gated.reshape(TOKENS, nblocks, block_width).transpose(1, 0, 2), residues.reshape(nblocks, block_width, M), pole_rates.reshape(nblocks, block_width, M))
    convolved = lax.map(filter_block, pieces).transpose(1, 0, 2).reshape(TOKENS, D)
    mixture = query_proj.astype(jnp.float32) * (convolved + skip_gain[None, :] * gated)
    scale = lax.rsqrt(lax.optimization_barrier(jnp.mean(mixture * mixture, axis=1)) + 1e-06)
    return (mixture * scale[:, None] * norm_gain[None, :]).astype(jnp.bfloat16)
```

```python
import functools

import jax
import jax.numpy as jnp
from jax import lax
from jax.experimental import pallas as pl
from jax.experimental.pallas import tpu as pltpu
from jax.sharding import PartitionSpec as P

MESH = pl.DeviceIdType.MESH
F32 = jnp.float32
LANES = 128
SUB = 8
OWNER_Z = (0, 7)


def shift_rows(x, n, rows):
    return jnp.where(rows >= n, pltpu.roll(x, n, 0), 0.0)


def body(
    length,
    q_hbm,
    k_hbm,
    v_hbm,
    res_hbm,
    rate_hbm,
    skip_hbm,
    gain_hbm,
    out_ref,
    q_ref,
    k_ref,
    v_ref,
    res_ref,
    rate_ref,
    skip_ref,
    gain_ref,
    g_ref,
    y_ref,
    q32_ref,
    ends_ref,
    local_ref,
    state_ref,
    lead_ref,
    square_ref,
    scale_ref,
    pieces_ref,
    prefix_ref,
    part_ref,
    parts_ref,
    load_sem,
    send_sem,
    piece_sem,
    back_sem,
    state_sem,
    part_send,
    part_sem,
):
    me = lax.axis_index("seq")
    chan = lax.axis_index("chan")
    tokens, channels = q_ref.shape
    modes = res_ref.shape[0]
    tiles = channels // LANES
    steps = tokens // SUB
    devices = pieces_ref.shape[0]
    chans = parts_ref.shape[0] + 1
    groups = devices // SUB
    x, z, core = me // 16, lax.rem(me // 2, 8), lax.rem(me, 2)
    is_owner = (z == OWNER_Z[0]) | (z == OWNER_Z[1])
    high = jnp.where(z == OWNER_Z[1], 1, 0)
    owned = core + 2 * x + 8 * high

    def owner_of(half, tile):
        return ((tile // 2) * 8 + OWNER_Z[half]) * 2 + lax.rem(tile, 2)

    loads = [
        pltpu.make_async_copy(src, dst, load_sem.at[n])
        for n, (src, dst) in enumerate(
            (
                (k_hbm, k_ref),
                (v_hbm, v_ref),
                (rate_hbm, rate_ref),
                (res_hbm, res_ref),
                (q_hbm, q_ref),
                (skip_hbm, skip_ref),
                (gain_hbm, gain_ref),
            )
        )
    ]
    for load in loads:
        load.start()

    barrier = pltpu.get_barrier_semaphore()

    @pl.when(is_owner)
    def _():
        def greet(n, carry):
            pl.semaphore_signal(
                barrier, inc=1, device_id={"seq": lax.rem(me + n, devices)}, device_id_type=MESH
            )
            return carry

        lax.fori_loop(1, devices, greet, 0)

    for n in range(1, chans):
        pl.semaphore_signal(
            barrier, inc=1, device_id={"chan": lax.rem(chan + n, chans)}, device_id_type=MESH
        )

    rows = lax.broadcasted_iota(jnp.int32, (SUB, LANES), 0)
    rows_f = rows.astype(F32)
    sub = tokens // SUB

    for load in loads[:3]:
        load.wait()

    def row(ref, m, cols):
        return jnp.broadcast_to(ref[m : m + 1, cols], (SUB, LANES))

    def block_ends(tile, carry):
        cols = pl.ds(pl.multiple_of(tile * LANES, LANES), LANES)
        g_ref[tile] = k_ref[:, cols].astype(F32) * v_ref[:, cols].astype(F32)
        rates = [row(rate_ref, m, cols) * (-1.0 / length) for m in range(modes)]
        decay = [jnp.exp(r) for r in rates]
        held = None
        for i in range(sub):
            g = g_ref[tile, pl.ds(i, SUB, stride=sub), :]
            held = [g] * modes if held is None else [h * a + g for h, a in zip(held, decay)]
        for m in range(modes):
            ends_ref[tile, m] = held[m]
            weight = jnp.exp(rates[m] * (sub * (SUB - 1.0 - rows_f)))
            local_ref[m : m + 1, cols] = jnp.sum(held[m] * weight, axis=0, keepdims=True)
        return carry

    lax.fori_loop(0, tiles, block_ends, 0)

    pl.semaphore_wait(barrier, chans - 1 + jnp.where(is_owner, 2 * tiles - 1, 2 * tiles))

    def send_pieces(tile, carry):
        cols = pl.ds(pl.multiple_of(tile * LANES, LANES), LANES)
        for half in range(2):
            piece = local_ref.at[half * SUB : (half + 1) * SUB, cols]
            owner = owner_of(half, tile)

            @pl.when(owner == me)
            def _():
                pltpu.make_async_copy(piece, pieces_ref.at[me], piece_sem.at[me // SUB]).start()

            @pl.when(owner != me)
            def _():
                pltpu.make_async_remote_copy(
                    src_ref=piece,
                    dst_ref=pieces_ref.at[me],
                    send_sem=send_sem,
                    recv_sem=piece_sem.at[me // SUB],
                    device_id={"seq": owner},
                    device_id_type=MESH,
                ).start()

        return carry

    lax.fori_loop(0, tiles, send_pieces, 0)

    for load in loads[3:]:
        load.wait()

    def local_part(tile, carry):
        cols = pl.ds(pl.multiple_of(tile * LANES, LANES), LANES)
        q32_ref[tile] = q_ref[:, cols].astype(F32)
        decay, weight, held = [], [], []
        for m in range(modes):
            rate = row(rate_ref, m, cols) * (-1.0 / length)
            weight.append(row(res_ref, m, cols))
            decay.append(jnp.exp(rate))
            lead_ref[tile, m] = weight[m] * jnp.exp(rate * (rows_f + 1.0))
            long = jnp.exp(rate * sub)
            ends = ends_ref[tile, m]
            ends = ends + long * shift_rows(ends, 1, rows)
            long = long * long
            ends = ends + long * shift_rows(ends, 2, rows)
            long = long * long
            ends = ends + long * shift_rows(ends, 4, rows)
            held.append(shift_rows(ends, 1, rows))
        skip = row(skip_ref, 0, cols)
        for i in range(sub):
            spots = pl.ds(i, SUB, stride=sub)
            g = g_ref[tile, spots, :]
            held = [h * a + g for h, a in zip(held, decay)]
            terms = [h * w for h, w in zip(held, weight)] + [skip * g]
            while len(terms) > 1:
                terms = [sum(terms[n : n + 2]) for n in range(0, len(terms), 2)]
            y_ref[tile, spots, :] = terms[0]
        return carry

    lax.fori_loop(0, tiles, local_part, 0)
    square_ref[...] = jnp.zeros_like(square_ref)

    @pl.when(is_owner)
    def _():
        half_rows = pl.ds(pl.multiple_of(high * SUB, SUB), SUB)
        cols = pl.ds(pl.multiple_of((core + 2 * x) * LANES, LANES), LANES)
        whole = jnp.exp(rate_ref[half_rows, cols] * (-float(tokens) / length))
        prefix_ref[0] = jnp.zeros((SUB, LANES), F32)

        def send_back(to):
            @pl.when(to == me)
            def _():
                pltpu.make_async_copy(
                    prefix_ref.at[to], state_ref.at[half_rows, cols], state_sem
                ).start()

            @pl.when(to != me)
            def _():
                pltpu.make_async_remote_copy(
                    src_ref=prefix_ref.at[to],
                    dst_ref=state_ref.at[half_rows, cols],
                    send_sem=back_sem,
                    recv_sem=state_sem,
                    device_id={"seq": to},
                    device_id_type=MESH,
                ).start()

        def group(n, total):
            mine = pieces_ref.at[pl.ds(n * SUB, SUB)]
            pltpu.make_async_copy(mine, mine, piece_sem.at[n]).wait()

            def one(j, total):
                p = n * SUB + j
                prefix_ref[p] = total
                send_back(p)
                return total * whole + pieces_ref[p]

            return lax.fori_loop(0, SUB, one, total)

        lax.fori_loop(0, groups, group, jnp.zeros((SUB, LANES), F32))

    pltpu.make_async_copy(state_ref, state_ref, state_sem).wait()

    def add_state(tile, carry):
        cols = pl.ds(pl.multiple_of(tile * LANES, LANES), LANES)
        eighth = [jnp.exp(row(rate_ref, m, cols) * (-float(SUB) / length)) for m in range(modes)]
        terms = [lead_ref[tile, m] * row(state_ref, m, cols) for m in range(modes)]
        for i in range(steps):
            spots = pl.ds(i * SUB, SUB)
            total = list(terms)
            while len(total) > 1:
                total = [total[n] + total[n + 1] for n in range(0, len(total), 2)]
            mixed = q32_ref[tile, spots, :] * (y_ref[tile, spots, :] + total[0])
            y_ref[tile, spots, :] = mixed
            square_ref[spots, :] += mixed * mixed
            if i + 1 < steps:
                terms = [t * a for t, a in zip(terms, eighth)]
        return carry

    lax.fori_loop(0, tiles, add_state, 0)

    lanes = lax.broadcasted_iota(jnp.int32, (SUB, LANES), 1)
    part = jnp.zeros((SUB, LANES), F32)
    for i in range(steps):
        sums = jnp.sum(square_ref[i * SUB : (i + 1) * SUB, :], axis=1, keepdims=True)
        part = jnp.where(lanes == i, sums, part)
    part_ref[...] = part
    for n in range(1, chans):
        pltpu.make_async_remote_copy(
            src_ref=part_ref,
            dst_ref=parts_ref.at[n - 1],
            send_sem=part_send,
            recv_sem=part_sem,
            device_id={"chan": lax.rem(chan + n, chans)},
            device_id_type=MESH,
        ).start()
    pltpu.make_async_copy(parts_ref, parts_ref, part_sem).wait()
    whole_sum = part
    for n in range(1, chans):
        whole_sum = whole_sum + parts_ref[n - 1]
    scale = lax.rsqrt(whole_sum * (1.0 / (channels * chans)) + 1e-06)
    for i in range(steps):
        scale_ref[i * SUB : (i + 1) * SUB, :] = jnp.broadcast_to(scale[:, i : i + 1], (SUB, LANES))

    def finish(tile, carry):
        cols = pl.ds(pl.multiple_of(tile * LANES, LANES), LANES)
        out_ref[:, cols] = (y_ref[tile] * scale_ref[...] * gain_ref[:, cols]).astype(out_ref.dtype)
        return carry

    lax.fori_loop(0, tiles, finish, 0)

    pltpu.make_async_copy(parts_ref, parts_ref, part_send).wait()

    @pl.when(is_owner)
    def _():
        sent = pieces_ref.at[pl.ds(0, 2 * tiles - 1)]
        pltpu.make_async_copy(sent, sent, send_sem).wait()
        back = pieces_ref.at[pl.ds(0, devices - 1)]
        pltpu.make_async_copy(back, back, back_sem).wait()

    @pl.when(jnp.logical_not(is_owner))
    def _():
        sent = pieces_ref.at[pl.ds(0, 2 * tiles)]
        pltpu.make_async_copy(sent, sent, send_sem).wait()


def per_device(devices, chans, q, k, v, residues, rates, skip, gain):
    tokens, channels = q.shape
    modes = residues.shape[1]
    tiles = channels // LANES
    bf16 = q.dtype
    inputs = (q, k, v, residues.T, rates.T, skip[None, :], gain[None, :])
    vmem = pltpu.VMEM
    return pl.pallas_call(
        functools.partial(body, float(tokens * devices)),
        out_shape=jax.ShapeDtypeStruct((tokens, channels), bf16),
        in_specs=[pl.BlockSpec(memory_space=pltpu.HBM)] * len(inputs),
        out_specs=pl.BlockSpec(memory_space=vmem),
        scratch_shapes=[
            vmem((tokens, channels), bf16),
            vmem((tokens, channels), bf16),
            vmem((tokens, channels), bf16),
            vmem((modes, channels), F32),
            vmem((modes, channels), F32),
            vmem((1, channels), F32),
            vmem((1, channels), F32),
            vmem((tiles, tokens, LANES), F32),
            vmem((tiles, tokens, LANES), F32),
            vmem((tiles, tokens, LANES), F32),
            vmem((tiles, modes, SUB, LANES), F32),
            vmem((modes, channels), F32),
            vmem((modes, channels), F32),
            vmem((tiles, modes, SUB, LANES), F32),
            vmem((tokens, LANES), F32),
            vmem((tokens, LANES), F32),
            vmem((devices, SUB, LANES), F32),
            vmem((devices, SUB, LANES), F32),
            vmem((SUB, LANES), F32),
            vmem((chans - 1, SUB, LANES), F32),
            pltpu.SemaphoreType.DMA((7,)),
            pltpu.SemaphoreType.DMA,
            pltpu.SemaphoreType.DMA((devices // SUB,)),
            pltpu.SemaphoreType.DMA,
            pltpu.SemaphoreType.DMA,
            pltpu.SemaphoreType.DMA,
            pltpu.SemaphoreType.DMA,
        ],
        compiler_params=pltpu.CompilerParams(
            collective_id=0, has_side_effects=True, vmem_limit_bytes=24 * 1024 * 1024
        ),
    )(*[pltpu.with_memory_space_constraint(a, pltpu.HBM) for a in inputs])


def solution(mesh):
    devices, chans = mesh.shape["seq"], mesh.shape["chan"]
    return jax.shard_map(
        functools.partial(per_device, devices, chans),
        mesh=mesh,
        in_specs=(
            P("seq", "chan"),
            P("seq", "chan"),
            P("seq", "chan"),
            P("chan", None),
            P("chan", None),
            P("chan"),
            P("chan"),
        ),
        out_specs=P("seq", "chan"),
        check_vma=False,
    )
```

```python
import functools

import jax
import jax.numpy as jnp
from jax import lax
from jax.experimental import pallas as pl
from jax.experimental.pallas import tpu as pltpu
from jax.sharding import PartitionSpec as P

MESH = pl.DeviceIdType.MESH
F32 = jnp.float32
LANES = 128
SUB = 8
OWNER_Z = (0, 1)


def shift_rows(x, n, rows):
    return jnp.where(rows >= n, pltpu.roll(x, n, 0), 0.0)


def body(
    length,
    q_hbm,
    k_hbm,
    v_hbm,
    res_hbm,
    rate_hbm,
    skip_hbm,
    gain_hbm,
    out_ref,
    q_ref,
    k_ref,
    v_ref,
    res_ref,
    rate_ref,
    skip_ref,
    gain_ref,
    decay_ref,
    g_ref,
    y_ref,
    q32_ref,
    ends_ref,
    lead_ref,
    local_ref,
    other_ref,
    chip_ref,
    state_ref,
    start_ref,
    square_ref,
    scale_ref,
    pieces_ref,
    prefix_ref,
    part_ref,
    parts_ref,
    load_sem,
    key_sem,
    value_sem,
    other_sem,
    send_sem,
    piece_sem,
    back_sem,
    state_sem,
    part_send,
    part_sem,
):
    me = lax.axis_index("seq")
    chan = lax.axis_index("chan")
    tokens, channels = q_ref.shape
    modes = res_ref.shape[0]
    tiles = channels // LANES
    steps = tokens // SUB
    sub = tokens // SUB
    chips = pieces_ref.shape[0]
    devices = 2 * chips
    chans = parts_ref.shape[0] + 1
    chip = me // 2
    x, z, core = me // 16, lax.rem(chip, 8), lax.rem(me, 2)
    is_owner = z == OWNER_Z[0]
    which = 0
    for n in range(1, len(OWNER_Z)):
        is_owner = is_owner | (z == OWNER_Z[n])
        which = jnp.where(z == OWNER_Z[n], n, which)
    depth = modes // len(OWNER_Z)
    pieces = len(OWNER_Z) * tiles
    own_tile = core + 2 * x

    def owner_of(n, tile):
        return ((tile // 2) * 8 + OWNER_Z[n]) * 2 + lax.rem(tile, 2)

    def far_first(n):
        pair = n // 2
        turn = jnp.where(pair == 0, 2, jnp.where(pair == 1, 1, jnp.where(pair == 2, 3, 0)))
        return lax.rem(x + turn, 4) * 2 + lax.rem(n, 2)

    def near_first(n):
        pair = n // 2
        turn = jnp.where(pair == 2, 3, jnp.where(pair == 3, 2, pair))
        return lax.rem(x + turn, 4) * 2 + lax.rem(n, 2)

    def lanes_of(tile, width=1):
        return pl.ds(pl.multiple_of(tile * LANES, LANES), width * LANES)

    def load(src, dst, sem):
        return pltpu.make_async_copy(src, dst, sem)

    rate_load = load(rate_hbm, rate_ref, load_sem.at[0])
    rate_load.start()

    def load_pair(pair):
        cols = lanes_of(far_first(2 * pair), 2)
        return (
            load(k_hbm.at[:, cols], k_ref.at[:, cols], key_sem.at[pair]),
            load(v_hbm.at[:, cols], v_ref.at[:, cols], value_sem.at[pair]),
        )

    for pair in range(tiles // 2):
        for copy in load_pair(pair):
            copy.start()
    late_loads = [
        load(src, dst, load_sem.at[n + 1])
        for n, (src, dst) in enumerate(
            ((res_hbm, res_ref), (q_hbm, q_ref), (skip_hbm, skip_ref), (gain_hbm, gain_ref))
        )
    ]
    for copy in late_loads:
        copy.start()

    barrier = pltpu.get_barrier_semaphore()

    @pl.when(is_owner)
    def _():
        def greet(n, carry):
            sender = lax.rem(chip + n, chips) * 2 + 1

            @pl.when(sender != me)
            def _():
                pl.semaphore_signal(
                    barrier, inc=1, device_id={"seq": sender}, device_id_type=MESH
                )

            return carry

        lax.fori_loop(0, chips, greet, 0)

    @pl.when(core == 1)
    def _():
        pl.semaphore_signal(barrier, inc=1, device_id={"seq": me - 1}, device_id_type=MESH)

    for n in range(1, chans):
        pl.semaphore_signal(
            barrier, inc=1, device_id={"chan": lax.rem(chan + n, chans)}, device_id_type=MESH
        )

    rows = lax.broadcasted_iota(jnp.int32, (SUB, LANES), 0)
    rows_f = rows.astype(F32)

    rate_load.wait()
    for n, power in enumerate((1, sub, 2 * sub, 4 * sub)):
        decay_ref[n] = jnp.exp(rate_ref[...] * (-float(power) / length))

    def row(ref, m, cols):
        return jnp.broadcast_to(ref[m : m + 1, cols], (SUB, LANES))

    greetings = jnp.where(core == 1, pieces - jnp.where(is_owner, 1, 0), 1)
    pl.semaphore_wait(barrier, chans - 1 + greetings)

    def block_ends(n, carry):
        tile = far_first(n)
        cols = lanes_of(tile)

        @pl.when(lax.rem(n, 2) == 0)
        def _():
            for copy in load_pair(n // 2):
                copy.wait()

        g_ref[tile] = k_ref[:, cols].astype(F32) * v_ref[:, cols].astype(F32)
        decay = [row(decay_ref.at[0], m, cols) for m in range(modes)]
        held = None
        for i in range(sub):
            g = g_ref[tile, pl.ds(i, SUB, stride=sub), :]
            held = [g] * modes if held is None else [h * a + g for h, a in zip(held, decay)]
        for m in range(modes):
            end = held[m]
            ends_ref[tile, m] = end
            end = end + row(decay_ref.at[1], m, cols) * pltpu.roll(end, 1, 0)
            end = end + row(decay_ref.at[2], m, cols) * pltpu.roll(end, 2, 0)
            end = end + row(decay_ref.at[3], m, cols) * pltpu.roll(end, 4, 0)
            local_ref[m : m + 1, cols] = end[SUB - 1 :]

        @pl.when(core == 0)
        def _():
            pltpu.make_async_remote_copy(
                src_ref=local_ref.at[:, cols],
                dst_ref=other_ref.at[:, cols],
                send_sem=send_sem,
                recv_sem=other_sem.at[tile],
                device_id={"seq": me + 1},
                device_id_type=MESH,
            ).start()

        return carry

    lax.fori_loop(0, tiles, block_ends, 0)

    decay_ref[4] = jnp.exp(rate_ref[...] * (-float(tokens) / length))

    @pl.when(core == 1)
    def _():
        def send_pieces(n, carry):
            tile = far_first(n)
            cols = lanes_of(tile)
            mine = other_ref.at[:, cols]
            pltpu.make_async_copy(mine, mine, other_sem.at[tile]).wait()
            chip_ref[:, cols] = other_ref[:, cols] * decay_ref[4, :, cols] + local_ref[:, cols]
            for n in range(len(OWNER_Z)):
                piece = chip_ref.at[n * depth : (n + 1) * depth, cols]
                owner = owner_of(n, tile)

                @pl.when(owner == me)
                def _():
                    pltpu.make_async_copy(
                        piece, pieces_ref.at[chip], piece_sem.at[chip // 4]
                    ).start()

                @pl.when(owner != me)
                def _():
                    pltpu.make_async_remote_copy(
                        src_ref=piece,
                        dst_ref=pieces_ref.at[chip],
                        send_sem=send_sem,
                        recv_sem=piece_sem.at[chip // 4],
                        device_id={"seq": owner},
                        device_id_type=MESH,
                    ).start()

            return carry

        lax.fori_loop(0, tiles, send_pieces, 0)

    for copy in late_loads:
        copy.wait()
    decay_ref[5] = jnp.exp(rate_ref[...] * (-float(SUB) / length))

    @pl.when(core == 0)
    def _():
        other_ref[...] = jnp.zeros_like(other_ref)

    def local_part(tile, carry):
        cols = lanes_of(tile)
        q32_ref[tile] = q_ref[:, cols].astype(F32)
        decay, weight, held = [], [], []
        for m in range(modes):
            rate = row(rate_ref, m, cols) * (-1.0 / length)
            weight.append(row(res_ref, m, cols))
            decay.append(row(decay_ref.at[0], m, cols))
            lead_ref[tile, m] = weight[m] * jnp.exp(rate * (rows_f + 1.0))
            ends = ends_ref[tile, m]
            ends = ends + row(decay_ref.at[1], m, cols) * shift_rows(ends, 1, rows)
            ends = ends + row(decay_ref.at[2], m, cols) * shift_rows(ends, 2, rows)
            ends = ends + row(decay_ref.at[3], m, cols) * shift_rows(ends, 4, rows)
            held.append(shift_rows(ends, 1, rows))
        skip = row(skip_ref, 0, cols)
        for i in range(sub):
            spots = pl.ds(i, SUB, stride=sub)
            g = g_ref[tile, spots, :]
            held = [h * a + g for h, a in zip(held, decay)]
            terms = [h * w for h, w in zip(held, weight)] + [skip * g]
            while len(terms) > 1:
                terms = [sum(terms[n : n + 2]) for n in range(0, len(terms), 2)]
            y_ref[tile, spots, :] = terms[0]
        return carry

    lax.fori_loop(0, tiles, local_part, 0)
    square_ref[...] = jnp.zeros_like(square_ref)

    @pl.when(is_owner)
    def _():
        mine = pl.ds(pl.multiple_of(which * depth, depth), depth)
        cols = lanes_of(own_tile)
        whole = rate_ref[0:depth, cols]
        for n in range(1, len(OWNER_Z)):
            whole = jnp.where(which == n, rate_ref[n * depth : (n + 1) * depth, cols], whole)
        whole = jnp.exp(whole * (-2.0 * tokens / length))

        def send_back(p, to):
            @pl.when(to == me)
            def _():
                pltpu.make_async_copy(
                    prefix_ref.at[p], state_ref.at[mine, cols], state_sem.at[own_tile]
                ).start()

            @pl.when(to != me)
            def _():
                pltpu.make_async_remote_copy(
                    src_ref=prefix_ref.at[p],
                    dst_ref=state_ref.at[mine, cols],
                    send_sem=back_sem,
                    recv_sem=state_sem.at[own_tile],
                    device_id={"seq": to},
                    device_id_type=MESH,
                ).start()

        def group(n, total):
            some = pieces_ref.at[pl.ds(n * 4, 4)]
            pltpu.make_async_copy(some, some, piece_sem.at[n]).wait()

            def one(j, total):
                p = n * 4 + j
                prefix_ref[p] = total
                send_back(p, 2 * p)
                send_back(p, 2 * p + 1)
                return total * whole + pieces_ref[p]

            return lax.fori_loop(0, 4, one, total)

        lax.fori_loop(0, chips // 4, group, jnp.zeros((depth, LANES), F32))

    def add_state(n, carry):
        tile = near_first(n)
        cols = lanes_of(tile)
        arrived = state_ref.at[:, cols]
        pltpu.make_async_copy(arrived, arrived, state_sem.at[tile]).wait()
        keep = jnp.where(core == 1, decay_ref[4, :, cols], 1.0)
        start_ref[...] = state_ref[:, cols] * keep + other_ref[:, cols]
        eighth = [row(decay_ref.at[5], m, cols) for m in range(modes)]
        terms = [
            lead_ref[tile, m] * jnp.broadcast_to(start_ref[m : m + 1], (SUB, LANES))
            for m in range(modes)
        ]
        for i in range(steps):
            spots = pl.ds(i * SUB, SUB)
            total = list(terms)
            while len(total) > 1:
                total = [total[n] + total[n + 1] for n in range(0, len(total), 2)]
            mixed = q32_ref[tile, spots, :] * (y_ref[tile, spots, :] + total[0])
            y_ref[tile, spots, :] = mixed
            square_ref[spots, :] += mixed * mixed
            if i + 1 < steps:
                terms = [t * a for t, a in zip(terms, eighth)]
        return carry

    lax.fori_loop(0, tiles, add_state, 0)

    lanes = lax.broadcasted_iota(jnp.int32, (SUB, LANES), 1)
    part = jnp.zeros((SUB, LANES), F32)
    for i in range(steps):
        sums = jnp.sum(square_ref[i * SUB : (i + 1) * SUB, :], axis=1, keepdims=True)
        part = jnp.where(lanes == i, sums, part)
    part_ref[...] = part
    for n in (2, 1, 3):
        pltpu.make_async_remote_copy(
            src_ref=part_ref,
            dst_ref=parts_ref.at[n - 1],
            send_sem=part_send,
            recv_sem=part_sem,
            device_id={"chan": lax.rem(chan + n, chans)},
            device_id_type=MESH,
        ).start()
    pltpu.make_async_copy(parts_ref, parts_ref, part_sem).wait()
    whole_sum = part
    for n in range(1, chans):
        whole_sum = whole_sum + parts_ref[n - 1]
    scale = lax.rsqrt(whole_sum * (1.0 / (channels * chans)) + 1e-06)
    for i in range(steps):
        scale_ref[i * SUB : (i + 1) * SUB, :] = jnp.broadcast_to(scale[:, i : i + 1], (SUB, LANES))

    def finish(tile, carry):
        cols = lanes_of(tile)
        out_ref[:, cols] = (y_ref[tile] * scale_ref[...] * gain_ref[:, cols]).astype(out_ref.dtype)
        return carry

    lax.fori_loop(0, tiles, finish, 0)

    pltpu.make_async_copy(parts_ref, parts_ref, part_send).wait()

    @pl.when(core == 0)
    def _():
        pltpu.make_async_copy(local_ref, local_ref, send_sem).wait()

    @pl.when((core == 1) & is_owner)
    def _():
        sent = pieces_ref.at[pl.ds(0, pieces - 1)]
        pltpu.make_async_copy(sent, sent, send_sem).wait()

    @pl.when((core == 1) & jnp.logical_not(is_owner))
    def _():
        sent = pieces_ref.at[pl.ds(0, pieces)]
        pltpu.make_async_copy(sent, sent, send_sem).wait()

    @pl.when(is_owner)
    def _():
        most = prefix_ref.at[pl.ds(0, chips - 1)]
        pltpu.make_async_copy(prefix_ref, prefix_ref, back_sem).wait()
        pltpu.make_async_copy(most, most, back_sem).wait()


def per_device(devices, chans, q, k, v, residues, rates, skip, gain):
    tokens, channels = q.shape
    modes = residues.shape[1]
    tiles = channels // LANES
    chips = devices // 2
    bf16 = q.dtype
    inputs = (q, k, v, residues.T, rates.T, skip[None, :], gain[None, :])
    vmem = pltpu.VMEM
    dma = pltpu.SemaphoreType.DMA
    whole = vmem((tokens, channels), bf16)
    table = vmem((modes, channels), F32)
    line = vmem((1, channels), F32)
    by_tile = vmem((tiles, tokens, LANES), F32)
    by_mode = vmem((tiles, modes, SUB, LANES), F32)
    by_token = vmem((tokens, LANES), F32)
    by_chip = vmem((chips, modes // len(OWNER_Z), LANES), F32)
    return pl.pallas_call(
        functools.partial(body, float(tokens * devices)),
        out_shape=jax.ShapeDtypeStruct((tokens, channels), bf16),
        in_specs=[pl.BlockSpec(memory_space=pltpu.HBM)] * len(inputs),
        out_specs=pl.BlockSpec(memory_space=vmem),
        scratch_shapes=[whole, whole, whole, table, table, line, line]
        + [vmem((6, modes, channels), F32)]
        + [by_tile, by_tile, by_tile, by_mode, by_mode]
        + [table, table, table, table, vmem((modes, LANES), F32), by_token, by_token]
        + [by_chip, by_chip]
        + [vmem((SUB, LANES), F32), vmem((chans - 1, SUB, LANES), F32)]
        + [dma((5,)), dma((tiles // 2,)), dma((tiles // 2,)), dma((tiles,)), dma]
        + [dma((chips // 4,)), dma, dma((tiles,)), dma, dma],
        compiler_params=pltpu.CompilerParams(
            collective_id=0, has_side_effects=True, vmem_limit_bytes=24 * 1024 * 1024
        ),
    )(*[pltpu.with_memory_space_constraint(a, pltpu.HBM) for a in inputs])


def solution(mesh):
    devices, chans = mesh.shape["seq"], mesh.shape["chan"]
    return jax.shard_map(
        functools.partial(per_device, devices, chans),
        mesh=mesh,
        in_specs=(
            P("seq", "chan"),
            P("seq", "chan"),
            P("seq", "chan"),
            P("chan", None),
            P("chan", None),
            P("chan"),
            P("chan"),
        ),
        out_specs=P("seq", "chan"),
        check_vma=False,
    )
```

```python
import functools

import jax
import jax.numpy as jnp
from jax import lax
from jax.experimental import pallas as pl
from jax.experimental.pallas import tpu as pltpu
from jax.sharding import PartitionSpec as P

MESH = pl.DeviceIdType.MESH
F32 = jnp.float32
LANES = 128
SUB = 8
OWNER_Z = (0, 1)
DIRECT_Z = 4
QUIET = 5
POWERS = (1, 2, 4, 8, 16, 32, 64, 128, 256)


def shift_rows(x, n, rows):
    return jnp.where(rows >= n, pltpu.roll(x, n, 0), 0.0)


def body(
    length,
    q_hbm,
    k_hbm,
    v_hbm,
    res_hbm,
    rate_hbm,
    skip_hbm,
    gain_hbm,
    out_ref,
    q_ref,
    k_ref,
    v_ref,
    res_ref,
    rate_ref,
    skip_ref,
    gain_ref,
    decay_ref,
    g_ref,
    sorted_ref,
    y_ref,
    q32_ref,
    ends_ref,
    lead_ref,
    local_ref,
    other_ref,
    chip_ref,
    state_ref,
    start_ref,
    square_ref,
    pieces_ref,
    prefix_ref,
    part_ref,
    parts_ref,
    load_sem,
    key_sem,
    value_sem,
    other_sem,
    pair_sem,
    send_sem,
    piece_sem,
    back_sem,
    state_sem,
    part_send,
    part_sem,
):
    me = lax.axis_index("seq")
    chan = lax.axis_index("chan")
    tokens, channels = q_ref.shape
    modes = res_ref.shape[0]
    tiles = channels // LANES
    steps = tokens // SUB
    sub = tokens // SUB
    chips = pieces_ref.shape[0]
    devices = 2 * chips
    chans = parts_ref.shape[0] + 1
    chip = me // 2
    x, z, core = me // 16, lax.rem(chip, 8), lax.rem(me, 2)
    is_owner = (z == OWNER_Z[0]) | (z == OWNER_Z[1])
    which = jnp.where(z == OWNER_Z[1], 1, 0)
    own_tile = 2 * x + core
    depth = modes // 2
    direct = z < DIRECT_Z

    def owner_of(half, tile):
        return ((tile // 2) * 8 + OWNER_Z[half]) * 2 + lax.rem(tile, 2)

    def far_first(n):
        pair = n // 2
        turn = jnp.where(pair == 0, 2, jnp.where(pair == 1, 1, jnp.where(pair == 2, 3, 0)))
        return lax.rem(x + turn, 4) * 2 + lax.rem(n, 2)

    def near_first(n):
        pair = n // 2
        turn = jnp.where(pair == 1, 3, jnp.where(pair == 2, 1, jnp.where(pair == 3, 2, 0)))
        return lax.rem(x + turn, 4) * 2 + lax.rem(n, 2)

    def lanes_of(tile, width=1):
        return pl.ds(pl.multiple_of(tile * LANES, LANES), width * LANES)

    def load(src, dst, sem):
        return pltpu.make_async_copy(src, dst, sem)

    rate_load = load(rate_hbm, rate_ref, load_sem.at[0])
    rate_load.start()

    def load_pair(pair):
        cols = lanes_of(far_first(2 * pair), 2)
        return (
            load(k_hbm.at[:, cols], k_ref.at[:, cols], key_sem.at[pair]),
            load(v_hbm.at[:, cols], v_ref.at[:, cols], value_sem.at[pair]),
        )

    for pair in range(tiles // 2):
        for copy in load_pair(pair):
            copy.start()
    late_loads = [
        load(src, dst, load_sem.at[n + 1])
        for n, (src, dst) in enumerate(
            ((res_hbm, res_ref), (q_hbm, q_ref), (skip_hbm, skip_ref), (gain_hbm, gain_ref))
        )
    ]
    for copy in late_loads:
        copy.start()

    barrier = pltpu.get_barrier_semaphore()

    @pl.when(is_owner)
    def _():
        def greet(n, carry):
            sender = lax.rem(chip + n, chips)

            @pl.when(2 * sender != me)
            def _():
                pl.semaphore_signal(
                    barrier, inc=1, device_id={"seq": 2 * sender}, device_id_type=MESH
                )

            return carry

        lax.fori_loop(0, chips, greet, 0)

    @pl.when(core == 0)
    def _():
        pl.semaphore_signal(barrier, inc=1, device_id={"seq": me + 1}, device_id_type=MESH)

    for n in range(1, chans):
        pl.semaphore_signal(
            barrier, inc=1, device_id={"chan": lax.rem(chan + n, chans)}, device_id_type=MESH
        )

    rows = lax.broadcasted_iota(jnp.int32, (SUB, LANES), 0)
    rows_f = rows.astype(F32)

    def set_decay(power):
        for tile in range(tiles):
            rate = rate_ref[:, tile * LANES : (tile + 1) * LANES]
            decay_ref[POWERS.index(power), tile] = jnp.exp(rate * (-float(power) / length))

    rate_load.wait()
    for power in (1, 2, 4, 8, 16):
        set_decay(power)

    def row(ref, m, cols):
        return jnp.broadcast_to(ref[m : m + 1, cols], (SUB, LANES))

    def decay_row(power, tile, m):
        return jnp.broadcast_to(decay_ref[POWERS.index(power), tile, m : m + 1], (SUB, LANES))


    def wait_pair(n):
        @pl.when(lax.rem(n, 2) == 0)
        def _():
            for copy in load_pair(n // 2):
                copy.wait()

    def run_block(n):
        tile = far_first(n)
        cols = lanes_of(tile)
        eighth = [decay_row(8, tile, m) for m in range(modes)]
        stride = [decay_row(16, tile, m) for m in range(modes)]
        held = None
        for i in range(0, tokens, 2 * SUB):
            spots = slice(i, i + 2 * SUB)
            g = k_ref[spots, cols].astype(F32) * v_ref[spots, cols].astype(F32)
            step = [g[:SUB] * a + g[SUB:] for a in eighth]
            held = step if held is None else [h * a + t for h, a, t in zip(held, stride, step)]
        for m in range(modes):
            ends_ref[tile, m] = held[m]

    def gather_rows(n):
        tile = far_first(n)
        for m in range(modes):
            end = ends_ref[tile, m]
            for power in (1, 2, 4):
                end = end + decay_row(power, tile, m) * pltpu.roll(end, power, 0)
            local_ref[tile, m : m + 1] = end[SUB - 1 :]

    def send_local(n):
        tile = far_first(n)

        @pl.when(core == 1)
        def _():
            pltpu.make_async_remote_copy(
                src_ref=local_ref.at[tile],
                dst_ref=other_ref.at[tile],
                send_sem=pair_sem,
                recv_sem=other_sem.at[tile],
                device_id={"seq": me - 1},
                device_id_type=MESH,
            ).start()

    def quiet_block(n, carry):
        wait_pair(n)
        gather_rows(n - 1)
        run_block(n)
        return carry

    def sending_block(n, carry):
        quiet_block(n, carry)
        send_local(n - 1)
        return carry

    def send_earlier(n, carry):
        send_local(n)
        return carry

    wait_pair(0)
    run_block(0)
    lax.fori_loop(1, QUIET, quiet_block, 0)
    sends = 2 * tiles - jnp.where(is_owner, 1, 0)
    pl.semaphore_wait(barrier, chans - 1 + jnp.where(core == 0, sends, 1))
    lax.fori_loop(0, QUIET - 1, send_earlier, 0)
    lax.fori_loop(QUIET, tiles, sending_block, 0)
    gather_rows(tiles - 1)
    send_local(tiles - 1)

    set_decay(tokens)

    @pl.when(core == 0)
    def _():
        def send_pieces(n, carry):
            tile = far_first(n)
            mine = other_ref.at[tile]
            pltpu.make_async_copy(mine, mine, other_sem.at[tile]).wait()
            chip_ref[tile] = local_ref[tile] * decay_ref[POWERS.index(tokens), tile] + other_ref[tile]
            for half in range(2):
                owner = owner_of(half, tile)
                piece = chip_ref.at[tile, half * depth : (half + 1) * depth]

                @pl.when((owner == me))
                def _():
                    pltpu.make_async_copy(
                        piece, pieces_ref.at[chip], piece_sem.at[chip // 4]
                    ).start()

                @pl.when((owner != me))
                def _():
                    pltpu.make_async_remote_copy(
                        src_ref=piece,
                        dst_ref=pieces_ref.at[chip],
                        send_sem=send_sem,
                        recv_sem=piece_sem.at[chip // 4],
                        device_id={"seq": owner},
                        device_id_type=MESH,
                    ).start()

            return carry

        lax.fori_loop(0, tiles, send_pieces, 0)
        pltpu.make_async_remote_copy(
            src_ref=local_ref,
            dst_ref=other_ref,
            send_sem=pair_sem,
            recv_sem=other_sem.at[0],
            device_id={"seq": me + 1},
            device_id_type=MESH,
        ).start()

    for copy in late_loads:
        copy.wait()
    for power in (32, 64, 128):
        set_decay(power)

    def local_part(tile, carry):
        cols = lanes_of(tile)
        q32_ref[tile] = q_ref[:, cols].astype(F32)
        g_ref[...] = k_ref[:, cols].astype(F32) * v_ref[:, cols].astype(F32)
        decay = [decay_row(1, tile, m) for m in range(modes)]
        stride = [decay_row(4, tile, m) for m in range(modes)]
        held = None
        for i in range(0, sub, 4):
            g = [g_ref[pl.ds(i + j, SUB, stride=sub), :] for j in range(4)]
            for j in range(4):
                sorted_ref[(i + j) * SUB : (i + j + 1) * SUB, :] = g[j]
            step = [((g[0] * a + g[1]) * a + g[2]) * a + g[3] for a in decay]
            held = step if held is None else [h * a + t for h, a, t in zip(held, stride, step)]
        for m in range(modes):
            rate = row(rate_ref, m, cols) * (-1.0 / length)
            lead_ref[tile, m] = row(res_ref, m, cols) * jnp.exp(rate * (rows_f + 1.0))
            for n in (1, 2, 4):
                held[m] = held[m] + decay_row(n * sub, tile, m) * shift_rows(held[m], n, rows)
            held[m] = shift_rows(held[m], 1, rows)
        weight = [row(res_ref, m, cols) for m in range(modes)]
        skip = row(skip_ref, 0, cols)
        for i in range(sub):
            spots = pl.ds(i, SUB, stride=sub)
            g = sorted_ref[i * SUB : (i + 1) * SUB, :]
            held = [h * a + g for h, a in zip(held, decay)]
            terms = [h * w for h, w in zip(held, weight)] + [skip * g]
            while len(terms) > 1:
                terms = [sum(terms[n : n + 2]) for n in range(0, len(terms), 2)]
            y_ref[tile, spots, :] = terms[0]
        return carry

    lax.fori_loop(0, tiles, local_part, 0)
    square_ref[...] = jnp.zeros_like(square_ref)

    @pl.when(is_owner)
    def _():
        mine = pl.ds(pl.multiple_of(which * depth, depth), depth)
        whole = jnp.exp(rate_ref[mine, lanes_of(own_tile)] * (-2.0 * tokens / length))

        def send_back(p, to):
            @pl.when(to == me)
            def _():
                pltpu.make_async_copy(
                    prefix_ref.at[p], state_ref.at[own_tile, mine], state_sem.at[own_tile]
                ).start()

            @pl.when(to != me)
            def _():
                pltpu.make_async_remote_copy(
                    src_ref=prefix_ref.at[p],
                    dst_ref=state_ref.at[own_tile, mine],
                    send_sem=back_sem,
                    recv_sem=state_sem.at[own_tile],
                    device_id={"seq": to},
                    device_id_type=MESH,
                ).start()

        def give(p, total):
            prefix_ref[p] = total
            send_back(p, 2 * p)

            @pl.when(lax.rem(p, 8) < DIRECT_Z)
            def _():
                send_back(p, 2 * p + 1)

        nothing = jnp.zeros((depth, LANES), F32)

        def group(n, total):
            some = pieces_ref.at[pl.ds(n * 4, 4)]
            pltpu.make_async_copy(some, some, piece_sem.at[n]).wait()
            give(n * 4, total)

            def one(j, total):
                p = n * 4 + j
                total = total * whole + pieces_ref[p]

                @pl.when(j < 3)
                def _():
                    give(p + 1, total)

                return total

            return lax.fori_loop(0, 4, one, total)

        lax.fori_loop(0, chips // 4, group, nothing)

    @pl.when(core == 1)
    def _():
        pltpu.make_async_copy(other_ref, other_ref, other_sem.at[0]).wait()

    def add_state(n, carry):
        tile = near_first(n)
        cols = lanes_of(tile)
        arrived = state_ref.at[tile]
        pltpu.make_async_copy(arrived, arrived, state_sem.at[tile]).wait()

        @pl.when((core == 0) & jnp.logical_not(direct))
        def _():
            pltpu.make_async_remote_copy(
                src_ref=state_ref.at[tile],
                dst_ref=state_ref.at[tile],
                send_sem=pair_sem,
                recv_sem=state_sem.at[tile],
                device_id={"seq": me + 1},
                device_id_type=MESH,
            ).start()

        state = state_ref[tile]
        start_ref[...] = jnp.where(core == 1, state * decay_ref[POWERS.index(tokens), tile] + other_ref[tile], state)
        gain = row(gain_ref, 0, cols)
        eighth = [decay_row(SUB, tile, m) for m in range(modes)]
        terms = [
            lead_ref[tile, m] * jnp.broadcast_to(start_ref[m : m + 1], (SUB, LANES))
            for m in range(modes)
        ]
        for i in range(steps):
            spots = pl.ds(i * SUB, SUB)
            total = list(terms)
            while len(total) > 1:
                total = [total[n] + total[n + 1] for n in range(0, len(total), 2)]
            mixed = q32_ref[tile, spots, :] * (y_ref[tile, spots, :] + total[0])
            y_ref[tile, spots, :] = mixed * gain
            square_ref[spots, :] += mixed * mixed
            if i + 1 < steps:
                terms = [t * a for t, a in zip(terms, eighth)]
        return carry

    lax.fori_loop(0, tiles, add_state, 0)

    lanes = lax.broadcasted_iota(jnp.int32, (SUB, LANES), 1)
    part = jnp.zeros((SUB, LANES), F32)
    for i in range(steps):
        sums = jnp.sum(square_ref[i * SUB : (i + 1) * SUB, :], axis=1, keepdims=True)
        part = jnp.where(lanes == i, sums, part)
    part_ref[...] = part
    for n in (2, 1, 3):
        pltpu.make_async_remote_copy(
            src_ref=part_ref,
            dst_ref=parts_ref.at[n - 1],
            send_sem=part_send,
            recv_sem=part_sem,
            device_id={"chan": lax.rem(chan + n, chans)},
            device_id_type=MESH,
        ).start()
    pltpu.make_async_copy(parts_ref, parts_ref, part_sem).wait()
    whole_sum = part
    for n in range(1, chans):
        whole_sum = whole_sum + parts_ref[n - 1]
    scale = lax.rsqrt(whole_sum * (1.0 / (channels * chans)) + 1e-06)
    for i in range(0, steps, 2):
        above = jnp.broadcast_to(scale[:, i : i + 1], (SUB, LANES))
        below = jnp.broadcast_to(scale[:, i + 1 : i + 2], (SUB, LANES))
        both = jnp.concatenate([above, below], axis=0)
        spots = slice(i * SUB, (i + 2) * SUB)
        for tile in range(tiles):
            cols = slice(tile * LANES, (tile + 1) * LANES)
            out_ref[spots, cols] = (y_ref[tile, spots, :] * both).astype(out_ref.dtype)

    pltpu.make_async_copy(parts_ref, parts_ref, part_send).wait()

    pltpu.make_async_copy(local_ref, local_ref, pair_sem).wait()

    @pl.when((core == 0) & jnp.logical_not(direct))
    def _():
        pltpu.make_async_copy(state_ref, state_ref, pair_sem).wait()

    def sent(count, sem):
        some = prefix_ref.at[pl.ds(0, count)]
        pltpu.make_async_copy(some, some, sem).wait()

    @pl.when((core == 0) & is_owner)
    def _():
        sent(2 * tiles - 1, send_sem)

    @pl.when((core == 0) & jnp.logical_not(is_owner))
    def _():
        sent(2 * tiles, send_sem)

    @pl.when(is_owner)
    def _():
        sent(chips - 1, back_sem)
        sent(4 * DIRECT_Z, back_sem)


def per_device(devices, chans, q, k, v, residues, rates, skip, gain):
    tokens, channels = q.shape
    modes = residues.shape[1]
    tiles = channels // LANES
    chips = devices // 2
    bf16 = q.dtype
    inputs = (q, k, v, residues.T, rates.T, skip[None, :], gain[None, :])
    vmem = pltpu.VMEM
    dma = pltpu.SemaphoreType.DMA
    whole = vmem((tokens, channels), bf16)
    table = vmem((modes, channels), F32)
    line = vmem((1, channels), F32)
    by_tile = vmem((tiles, tokens, LANES), F32)
    by_mode = vmem((tiles, modes, SUB, LANES), F32)
    by_token = vmem((tokens, LANES), F32)
    by_chip = vmem((chips, modes // 2, LANES), F32)
    packed = vmem((tiles, modes, LANES), F32)
    return pl.pallas_call(
        functools.partial(body, float(tokens * devices)),
        out_shape=jax.ShapeDtypeStruct((tokens, channels), bf16),
        in_specs=[pl.BlockSpec(memory_space=pltpu.HBM)] * len(inputs),
        out_specs=pl.BlockSpec(memory_space=vmem),
        scratch_shapes=[whole, whole, whole, table, table, line, line]
        + [vmem((len(POWERS), tiles, modes, LANES), F32)]
        + [by_token, by_token, by_tile, by_tile, by_mode, by_mode]
        + [packed, packed, packed, packed, vmem((modes, LANES), F32), by_token]
        + [by_chip, by_chip]
        + [vmem((SUB, LANES), F32), vmem((chans - 1, SUB, LANES), F32)]
        + [dma((5,)), dma((tiles // 2,)), dma((tiles // 2,)), dma((tiles,)), dma, dma]
        + [dma((chips // 4,)), dma, dma((tiles,)), dma, dma],
        compiler_params=pltpu.CompilerParams(
            collective_id=0, has_side_effects=True, vmem_limit_bytes=24 * 1024 * 1024
        ),
    )(*[pltpu.with_memory_space_constraint(a, pltpu.HBM) for a in inputs])


def solution(mesh):
    devices, chans = mesh.shape["seq"], mesh.shape["chan"]
    return jax.shard_map(
        functools.partial(per_device, devices, chans),
        mesh=mesh,
        in_specs=(
            P("seq", "chan"),
            P("seq", "chan"),
            P("seq", "chan"),
            P("chan", None),
            P("chan", None),
            P("chan"),
            P("chan"),
        ),
        out_specs=P("seq", "chan"),
        check_vma=False,
    )
```

```python
import functools

import jax
import jax.numpy as jnp
from jax import lax
from jax.experimental import pallas as pl
from jax.experimental.pallas import tpu as pltpu
from jax.sharding import PartitionSpec as P

MESH = pl.DeviceIdType.MESH
F32 = jnp.float32
LANES = 128
SUB = 8
OWNER_Z = (0, 1)
DIRECT_Z = 4
QUIET = 4
POWERS = (1, 2, 4, 8, 16, 32, 64, 128, 256)


def shift_rows(x, n, rows):
    return jnp.where(rows >= n, pltpu.roll(x, n, 0), 0.0)


def body(
    length,
    q_hbm,
    k_hbm,
    v_hbm,
    res_hbm,
    rate_hbm,
    skip_hbm,
    gain_hbm,
    out_ref,
    q_ref,
    k_ref,
    v_ref,
    res_ref,
    rate_ref,
    skip_ref,
    gain_ref,
    decay_ref,
    g_ref,
    sorted_ref,
    y_ref,
    q32_ref,
    ends_ref,
    lead_ref,
    local_ref,
    other_ref,
    chip_ref,
    state_ref,
    start_ref,
    square_ref,
    pieces_ref,
    prefix_ref,
    part_ref,
    parts_ref,
    load_sem,
    key_sem,
    value_sem,
    other_sem,
    pair_sem,
    send_sem,
    piece_sem,
    back_sem,
    state_sem,
    part_send,
    part_sem,
):
    me = lax.axis_index("seq")
    chan = lax.axis_index("chan")
    tokens, channels = q_ref.shape
    modes = res_ref.shape[0]
    tiles = channels // LANES
    steps = tokens // SUB
    sub = tokens // SUB
    chips = pieces_ref.shape[0]
    groups = chips // 4
    chans = parts_ref.shape[0] + 1
    chip = me // 2
    x, z, core = me // 16, lax.rem(chip, 8), lax.rem(me, 2)
    parties = len(OWNER_Z)
    is_owner = (z == OWNER_Z[0]) | (z == OWNER_Z[-1])
    which = jnp.where(z == OWNER_Z[0], 0, parties - 1)
    own_tile = 2 * x + core
    depth = modes // parties
    direct = z < DIRECT_Z

    def owner_of(half, tile):
        return ((tile // 2) * 8 + OWNER_Z[half]) * 2 + lax.rem(tile, 2)

    def far_first(n):
        pair = n // 2
        turn = jnp.where(pair == 0, 2, jnp.where(pair == 1, 3, jnp.where(pair == 2, 1, 0)))
        return lax.rem(x + turn, 4) * 2 + lax.rem(n, 2)

    def near_first(n):
        pair = n // 2
        turn = jnp.where(pair == 1, 3, jnp.where(pair == 2, 1, jnp.where(pair == 3, 2, 0)))
        return lax.rem(x + turn, 4) * 2 + lax.rem(n, 2)

    def lanes_of(tile, width=1):
        return pl.ds(pl.multiple_of(tile * LANES, LANES), width * LANES)

    def load(src, dst, sem):
        return pltpu.make_async_copy(src, dst, sem)

    def load_pair(pair):
        cols = lanes_of(far_first(2 * pair), 2)
        return (
            load(k_hbm.at[:, cols], k_ref.at[:, cols], key_sem.at[pair]),
            load(v_hbm.at[:, cols], v_ref.at[:, cols], value_sem.at[pair]),
        )

    rate_load = load(rate_hbm, rate_ref, load_sem.at[0])
    rate_load.start()
    for pair in range(tiles // 2):
        for copy in load_pair(pair):
            copy.start()

    barrier = pltpu.get_barrier_semaphore()

    @pl.when(is_owner)
    def _():
        def greet(n, carry):
            sender = lax.rem(chip + n, chips)

            @pl.when(2 * sender != me)
            def _():
                pl.semaphore_signal(
                    barrier, inc=1, device_id={"seq": 2 * sender}, device_id_type=MESH
                )

            return carry

        lax.fori_loop(0, chips, greet, 0)

    @pl.when(core == 0)
    def _():
        pl.semaphore_signal(barrier, inc=1, device_id={"seq": me + 1}, device_id_type=MESH)

    for n in range(1, chans):
        pl.semaphore_signal(
            barrier, inc=1, device_id={"chan": lax.rem(chan + n, chans)}, device_id_type=MESH
        )

    rows = lax.broadcasted_iota(jnp.int32, (SUB, LANES), 0)
    rows_f = rows.astype(F32)

    def set_decay(power):
        for tile in range(tiles):
            rate = rate_ref[:, tile * LANES : (tile + 1) * LANES]
            decay_ref[POWERS.index(power), tile] = jnp.exp(rate * (-float(power) / length))

    rate_load.wait()
    for power in (1, 2, 4, 8, 16, tokens):
        set_decay(power)

    def row(ref, m, cols):
        return jnp.broadcast_to(ref[m : m + 1, cols], (SUB, LANES))

    def decay_row(power, tile, m):
        return jnp.broadcast_to(decay_ref[POWERS.index(power), tile, m : m + 1], (SUB, LANES))


    def wait_pair(n):
        @pl.when(lax.rem(n, 2) == 0)
        def _():
            for copy in load_pair(n // 2):
                copy.wait()

    def run_block(n):
        tile = far_first(n)
        cols = lanes_of(tile)
        eighth = [decay_row(8, tile, m) for m in range(modes)]
        stride = [decay_row(16, tile, m) for m in range(modes)]
        held = None
        for i in range(0, tokens, 2 * SUB):
            spots = slice(i, i + 2 * SUB)
            g = k_ref[spots, cols].astype(F32) * v_ref[spots, cols].astype(F32)
            step = [g[:SUB] * a + g[SUB:] for a in eighth]
            held = step if held is None else [h * a + t for h, a, t in zip(held, stride, step)]
        for m in range(modes):
            ends_ref[tile, m] = held[m]

    def gather_rows(n):
        tile = far_first(n)
        for m in range(modes):
            end = ends_ref[tile, m]
            for power in (1, 2, 4):
                end = end + decay_row(power, tile, m) * pltpu.roll(end, power, 0)
            local_ref[tile, m : m + 1] = end[SUB - 1 :]

    def send_local(n):
        tile = far_first(n)

        @pl.when(core == 1)
        def _():
            pltpu.make_async_remote_copy(
                src_ref=local_ref.at[tile],
                dst_ref=other_ref.at[tile],
                send_sem=pair_sem,
                recv_sem=other_sem.at[tile],
                device_id={"seq": me - 1},
                device_id_type=MESH,
            ).start()

    def send_piece(n, carry):
        tile = far_first(n)
        mine = other_ref.at[tile]
        pltpu.make_async_copy(mine, mine, other_sem.at[tile]).wait()
        chip_ref[tile] = local_ref[tile] * decay_ref[POWERS.index(tokens), tile] + other_ref[tile]
        for half in range(parties):
            owner = owner_of(half, tile)
            piece = chip_ref.at[tile, half * depth : (half + 1) * depth]

            @pl.when(owner == me)
            def _():
                pltpu.make_async_copy(piece, pieces_ref.at[chip], piece_sem.at[chip // 4]).start()

            @pl.when(owner != me)
            def _():
                pltpu.make_async_remote_copy(
                    src_ref=piece,
                    dst_ref=pieces_ref.at[chip],
                    send_sem=send_sem,
                    recv_sem=piece_sem.at[chip // 4],
                    device_id={"seq": owner},
                    device_id_type=MESH,
                ).start()

        return carry

    def quiet_block(n, carry):
        wait_pair(n)
        gather_rows(n - 1)
        run_block(n)
        return carry

    def sending_block(n, carry):
        quiet_block(n, carry)
        send_local(n - 1)

        @pl.when(core == 0)
        def _():
            send_piece(n - QUIET, 0)

        return carry

    def send_earlier(n, carry):
        send_local(n)
        return carry

    late_loads = [
        load(src, dst, load_sem.at[n + 1])
        for n, (src, dst) in enumerate(
            ((res_hbm, res_ref), (q_hbm, q_ref), (skip_hbm, skip_ref), (gain_hbm, gain_ref))
        )
    ]
    for copy in late_loads:
        copy.start()
    wait_pair(0)
    run_block(0)
    lax.fori_loop(1, QUIET, quiet_block, 0)
    sends = parties * tiles - jnp.where(is_owner, 1, 0)
    pl.semaphore_wait(barrier, chans - 1 + jnp.where(core == 0, sends, 1))
    lax.fori_loop(0, QUIET - 1, send_earlier, 0)
    lax.fori_loop(QUIET, tiles, sending_block, 0)
    gather_rows(tiles - 1)
    send_local(tiles - 1)

    @pl.when(core == 0)
    def _():
        lax.fori_loop(tiles - QUIET, tiles, send_piece, 0)
        pltpu.make_async_remote_copy(
            src_ref=local_ref,
            dst_ref=other_ref,
            send_sem=pair_sem,
            recv_sem=other_sem.at[0],
            device_id={"seq": me + 1},
            device_id_type=MESH,
        ).start()

    for copy in late_loads:
        copy.wait()
    for power in (32, 64, 128):
        set_decay(power)

    def local_part(tile, carry):
        cols = lanes_of(tile)
        q32_ref[tile] = q_ref[:, cols].astype(F32)
        g_ref[...] = k_ref[:, cols].astype(F32) * v_ref[:, cols].astype(F32)
        decay = [decay_row(1, tile, m) for m in range(modes)]
        stride = [decay_row(4, tile, m) for m in range(modes)]
        held = None
        for i in range(0, sub, 4):
            g = [g_ref[pl.ds(i + j, SUB, stride=sub), :] for j in range(4)]
            for j in range(4):
                sorted_ref[(i + j) * SUB : (i + j + 1) * SUB, :] = g[j]
            step = [((g[0] * a + g[1]) * a + g[2]) * a + g[3] for a in decay]
            held = step if held is None else [h * a + t for h, a, t in zip(held, stride, step)]
        for m in range(modes):
            rate = row(rate_ref, m, cols) * (-1.0 / length)
            lead_ref[tile, m] = row(res_ref, m, cols) * jnp.exp(rate * (rows_f + 1.0))
            for n in (1, 2, 4):
                held[m] = held[m] + decay_row(n * sub, tile, m) * shift_rows(held[m], n, rows)
            held[m] = shift_rows(held[m], 1, rows)
        weight = [row(res_ref, m, cols) for m in range(modes)]
        skip = row(skip_ref, 0, cols)
        for i in range(sub):
            spots = pl.ds(i, SUB, stride=sub)
            g = sorted_ref[i * SUB : (i + 1) * SUB, :]
            held = [h * a + g for h, a in zip(held, decay)]
            terms = [h * w for h, w in zip(held, weight)] + [skip * g]
            while len(terms) > 1:
                terms = [sum(terms[n : n + 2]) for n in range(0, len(terms), 2)]
            y_ref[tile, spots, :] = terms[0]
        return carry

    lax.fori_loop(0, tiles, local_part, 0)
    square_ref[...] = jnp.zeros_like(square_ref)

    @pl.when(is_owner)
    def _():
        mine = pl.ds(pl.multiple_of(which * depth, depth), depth)
        whole = jnp.exp(rate_ref[mine, lanes_of(own_tile)] * (-2.0 * tokens / length))

        def send_back(p, to):
            @pl.when(to == me)
            def _():
                pltpu.make_async_copy(
                    prefix_ref.at[p], state_ref.at[own_tile, mine], state_sem.at[own_tile]
                ).start()

            @pl.when(to != me)
            def _():
                pltpu.make_async_remote_copy(
                    src_ref=prefix_ref.at[p],
                    dst_ref=state_ref.at[own_tile, mine],
                    send_sem=back_sem,
                    recv_sem=state_sem.at[own_tile],
                    device_id={"seq": to},
                    device_id_type=MESH,
                ).start()

        def give_group(n):
            for j in range(4):
                p = n * 4 + j
                send_back(p, 2 * p)

                @pl.when(lax.rem(p, 8) < DIRECT_Z)
                def _():
                    send_back(p, 2 * p + 1)

        def take_group(n, total):
            for j in range(4):
                prefix_ref[n * 4 + j] = total
                total = total * whole + pieces_ref[n * 4 + j]
            return total

        def await_group(n):
            some = pieces_ref.at[pl.ds(n * 4, 4)]
            pltpu.make_async_copy(some, some, piece_sem.at[n]).wait()

        for line in range(groups // 2):
            await_group(2 * line)

        def one_line(line, total):
            total = take_group(2 * line, total)
            give_group(2 * line)

            @pl.when(line > 0)
            def _():
                give_group(2 * line - 1)

            await_group(2 * line + 1)
            return take_group(2 * line + 1, total)

        lax.fori_loop(0, groups // 2, one_line, jnp.zeros((depth, LANES), F32))
        give_group(groups - 1)

    @pl.when(core == 1)
    def _():
        pltpu.make_async_copy(other_ref, other_ref, other_sem.at[0]).wait()

    def add_state(n, carry):
        tile = near_first(n)
        cols = lanes_of(tile)
        arrived = state_ref.at[tile]
        pltpu.make_async_copy(arrived, arrived, state_sem.at[tile]).wait()

        @pl.when((core == 0) & jnp.logical_not(direct))
        def _():
            pltpu.make_async_remote_copy(
                src_ref=state_ref.at[tile],
                dst_ref=state_ref.at[tile],
                send_sem=pair_sem,
                recv_sem=state_sem.at[tile],
                device_id={"seq": me + 1},
                device_id_type=MESH,
            ).start()

        state = state_ref[tile]
        start_ref[...] = jnp.where(core == 1, state * decay_ref[POWERS.index(tokens), tile] + other_ref[tile], state)
        gain = row(gain_ref, 0, cols)
        eighth = [decay_row(SUB, tile, m) for m in range(modes)]
        terms = [
            lead_ref[tile, m] * jnp.broadcast_to(start_ref[m : m + 1], (SUB, LANES))
            for m in range(modes)
        ]
        for i in range(steps):
            spots = pl.ds(i * SUB, SUB)
            total = list(terms)
            while len(total) > 1:
                total = [total[n] + total[n + 1] for n in range(0, len(total), 2)]
            mixed = q32_ref[tile, spots, :] * (y_ref[tile, spots, :] + total[0])
            y_ref[tile, spots, :] = mixed * gain
            square_ref[spots, :] += mixed * mixed
            if i + 1 < steps:
                terms = [t * a for t, a in zip(terms, eighth)]
        return carry

    lax.fori_loop(0, tiles, add_state, 0)

    lanes = lax.broadcasted_iota(jnp.int32, (SUB, LANES), 1)
    part = jnp.zeros((SUB, LANES), F32)
    for i in range(steps):
        sums = jnp.sum(square_ref[i * SUB : (i + 1) * SUB, :], axis=1, keepdims=True)
        part = jnp.where(lanes == i, sums, part)
    part_ref[...] = part
    for n in (2, 1, 3):
        pltpu.make_async_remote_copy(
            src_ref=part_ref,
            dst_ref=parts_ref.at[n - 1],
            send_sem=part_send,
            recv_sem=part_sem,
            device_id={"chan": lax.rem(chan + n, chans)},
            device_id_type=MESH,
        ).start()
    pltpu.make_async_copy(parts_ref, parts_ref, part_sem).wait()
    whole_sum = part
    for n in range(1, chans):
        whole_sum = whole_sum + parts_ref[n - 1]
    scale = lax.rsqrt(whole_sum * (1.0 / (channels * chans)) + 1e-06)
    for i in range(0, steps, 2):
        above = jnp.broadcast_to(scale[:, i : i + 1], (SUB, LANES))
        below = jnp.broadcast_to(scale[:, i + 1 : i + 2], (SUB, LANES))
        both = jnp.concatenate([above, below], axis=0)
        spots = slice(i * SUB, (i + 2) * SUB)
        for tile in range(tiles):
            cols = slice(tile * LANES, (tile + 1) * LANES)
            out_ref[spots, cols] = (y_ref[tile, spots, :] * both).astype(out_ref.dtype)

    pltpu.make_async_copy(parts_ref, parts_ref, part_send).wait()

    pltpu.make_async_copy(local_ref, local_ref, pair_sem).wait()

    @pl.when((core == 0) & jnp.logical_not(direct))
    def _():
        pltpu.make_async_copy(state_ref, state_ref, pair_sem).wait()

    def sent(count, sem):
        some = prefix_ref.at[pl.ds(0, count)]
        pltpu.make_async_copy(some, some, sem).wait()

    @pl.when((core == 0) & is_owner)
    def _():
        sent(parties * tiles - 1, send_sem)

    @pl.when((core == 0) & jnp.logical_not(is_owner))
    def _():
        sent(parties * tiles, send_sem)

    @pl.when(is_owner)
    def _():
        sent(chips - 1, back_sem)
        sent(4 * DIRECT_Z, back_sem)


def per_device(devices, chans, q, k, v, residues, rates, skip, gain):
    tokens, channels = q.shape
    modes = residues.shape[1]
    tiles = channels // LANES
    chips = devices // 2
    bf16 = q.dtype
    inputs = (q, k, v, residues.T, rates.T, skip[None, :], gain[None, :])
    vmem = pltpu.VMEM
    dma = pltpu.SemaphoreType.DMA
    whole = vmem((tokens, channels), bf16)
    table = vmem((modes, channels), F32)
    line = vmem((1, channels), F32)
    by_tile = vmem((tiles, tokens, LANES), F32)
    by_mode = vmem((tiles, modes, SUB, LANES), F32)
    by_token = vmem((tokens, LANES), F32)
    by_chip = vmem((chips, modes // len(OWNER_Z), LANES), F32)
    packed = vmem((tiles, modes, LANES), F32)
    return pl.pallas_call(
        functools.partial(body, float(tokens * devices)),
        out_shape=jax.ShapeDtypeStruct((tokens, channels), bf16),
        in_specs=[pl.BlockSpec(memory_space=pltpu.HBM)] * len(inputs),
        out_specs=pl.BlockSpec(memory_space=vmem),
        scratch_shapes=[whole, whole, whole, table, table, line, line]
        + [vmem((len(POWERS), tiles, modes, LANES), F32)]
        + [by_token, by_token, by_tile, by_tile, by_mode, by_mode]
        + [packed, packed, packed, packed, vmem((modes, LANES), F32), by_token]
        + [by_chip, by_chip]
        + [vmem((SUB, LANES), F32), vmem((chans - 1, SUB, LANES), F32)]
        + [dma((5,)), dma((tiles // 2,)), dma((tiles // 2,)), dma((tiles,)), dma, dma]
        + [dma((chips // 4,)), dma, dma((tiles,)), dma, dma],
        compiler_params=pltpu.CompilerParams(
            collective_id=0, has_side_effects=True, vmem_limit_bytes=24 * 1024 * 1024
        ),
    )(*[pltpu.with_memory_space_constraint(a, pltpu.HBM) for a in inputs])


def solution(mesh):
    devices, chans = mesh.shape["seq"], mesh.shape["chan"]
    return jax.shard_map(
        functools.partial(per_device, devices, chans),
        mesh=mesh,
        in_specs=(
            P("seq", "chan"),
            P("seq", "chan"),
            P("seq", "chan"),
            P("chan", None),
            P("chan", None),
            P("chan"),
            P("chan"),
        ),
        out_specs=P("seq", "chan"),
        check_vma=False,
    )
```

```python
import functools

import jax
import jax.numpy as jnp
from jax import lax
from jax.experimental import pallas as pl
from jax.experimental.pallas import tpu as pltpu
from jax.sharding import PartitionSpec as P

MESH = pl.DeviceIdType.MESH
F32 = jnp.float32
LANES = 128
SUB = 8
OWNER_Z = (0, 1)
DIRECT_Z = 3
QUIET = 4
POWERS = (1, 2, 4, 8, 16, 32, 64, 128, 256)


def shift_rows(x, n, rows):
    return jnp.where(rows >= n, pltpu.roll(x, n, 0), 0.0)


def body(
    length,
    q_hbm,
    k_hbm,
    v_hbm,
    res_hbm,
    rate_hbm,
    skip_hbm,
    gain_hbm,
    out_ref,
    q_ref,
    k_ref,
    v_ref,
    res_ref,
    rate_ref,
    skip_ref,
    gain_ref,
    decay_ref,
    g_ref,
    sorted_ref,
    y_ref,
    q32_ref,
    ends_ref,
    lead_ref,
    local_ref,
    other_ref,
    chip_ref,
    state_ref,
    start_ref,
    square_ref,
    pieces_ref,
    prefix_ref,
    part_ref,
    parts_ref,
    load_sem,
    key_sem,
    value_sem,
    other_sem,
    pair_sem,
    send_sem,
    piece_sem,
    back_sem,
    state_sem,
    part_send,
    part_sem,
):
    me = lax.axis_index("seq")
    chan = lax.axis_index("chan")
    tokens, channels = q_ref.shape
    modes = res_ref.shape[0]
    tiles = channels // LANES
    steps = tokens // SUB
    sub = tokens // SUB
    chips = pieces_ref.shape[0]
    groups = chips // 4
    chans = parts_ref.shape[0] + 1
    chip = me // 2
    x, z, core = me // 16, lax.rem(chip, 8), lax.rem(me, 2)
    parties = len(OWNER_Z)
    is_owner = (z == OWNER_Z[0]) | (z == OWNER_Z[-1])
    which = jnp.where(z == OWNER_Z[0], 0, parties - 1)
    own_tile = 2 * x + core
    depth = modes // parties
    direct = z < DIRECT_Z

    def owner_of(half, tile):
        return ((tile // 2) * 8 + OWNER_Z[half]) * 2 + lax.rem(tile, 2)

    def far_first(n):
        pair = n // 2
        turn = jnp.where(pair == 0, 2, jnp.where(pair == 1, 3, jnp.where(pair == 2, 1, 0)))
        return lax.rem(x + turn, 4) * 2 + lax.rem(n, 2)

    def near_first(n):
        pair = n // 2
        turn = jnp.where(pair == 1, 3, jnp.where(pair == 2, 1, jnp.where(pair == 3, 2, 0)))
        return lax.rem(x + turn, 4) * 2 + lax.rem(n, 2)

    def lanes_of(tile, width=1):
        return pl.ds(pl.multiple_of(tile * LANES, LANES), width * LANES)

    def load(src, dst, sem):
        return pltpu.make_async_copy(src, dst, sem)

    def load_pair(pair):
        cols = lanes_of(far_first(2 * pair), 2)
        return (
            load(k_hbm.at[:, cols], k_ref.at[:, cols], key_sem.at[pair]),
            load(v_hbm.at[:, cols], v_ref.at[:, cols], value_sem.at[pair]),
        )

    rate_load = load(rate_hbm, rate_ref, load_sem.at[0])
    rate_load.start()
    for pair in range(tiles // 2):
        for copy in load_pair(pair):
            copy.start()

    barrier = pltpu.get_barrier_semaphore()

    @pl.when(is_owner)
    def _():
        def greet(n, carry):
            sender = lax.rem(chip + n, chips)

            @pl.when(2 * sender != me)
            def _():
                pl.semaphore_signal(
                    barrier, inc=1, device_id={"seq": 2 * sender}, device_id_type=MESH
                )

            return carry

        lax.fori_loop(0, chips, greet, 0)

    @pl.when(core == 0)
    def _():
        pl.semaphore_signal(barrier, inc=1, device_id={"seq": me + 1}, device_id_type=MESH)

    for n in range(1, chans):
        pl.semaphore_signal(
            barrier, inc=1, device_id={"chan": lax.rem(chan + n, chans)}, device_id_type=MESH
        )

    rows = lax.broadcasted_iota(jnp.int32, (SUB, LANES), 0)
    rows_f = rows.astype(F32)

    def set_decay(power):
        for tile in range(tiles):
            rate = rate_ref[:, tile * LANES : (tile + 1) * LANES]
            decay_ref[POWERS.index(power), tile] = jnp.exp(rate * (-float(power) / length))

    rate_load.wait()
    for power in (1, 2, 4, 8, 16, tokens):
        set_decay(power)

    def row(ref, m, cols):
        return jnp.broadcast_to(ref[m : m + 1, cols], (SUB, LANES))

    def decay_row(power, tile, m):
        return jnp.broadcast_to(decay_ref[POWERS.index(power), tile, m : m + 1], (SUB, LANES))


    def wait_pair(n):
        @pl.when(lax.rem(n, 2) == 0)
        def _():
            for copy in load_pair(n // 2):
                copy.wait()

    def run_block(n):
        tile = far_first(n)
        cols = lanes_of(tile)
        eighth = [decay_row(8, tile, m) for m in range(modes)]
        stride = [decay_row(16, tile, m) for m in range(modes)]
        held = None
        for i in range(0, tokens, 2 * SUB):
            spots = slice(i, i + 2 * SUB)
            g = k_ref[spots, cols].astype(F32) * v_ref[spots, cols].astype(F32)
            step = [g[:SUB] * a + g[SUB:] for a in eighth]
            held = step if held is None else [h * a + t for h, a, t in zip(held, stride, step)]
        for m in range(modes):
            ends_ref[tile, m] = held[m]

    def gather_rows(n):
        tile = far_first(n)
        for m in range(modes):
            end = ends_ref[tile, m]
            for power in (1, 2, 4):
                end = end + decay_row(power, tile, m) * pltpu.roll(end, power, 0)
            local_ref[tile, m : m + 1] = end[SUB - 1 :]

    def send_local(n):
        tile = far_first(n)

        @pl.when(core == 1)
        def _():
            pltpu.make_async_remote_copy(
                src_ref=local_ref.at[tile],
                dst_ref=other_ref.at[tile],
                send_sem=pair_sem,
                recv_sem=other_sem.at[tile],
                device_id={"seq": me - 1},
                device_id_type=MESH,
            ).start()

    def send_piece(n, carry):
        tile = far_first(n)
        mine = other_ref.at[tile]
        pltpu.make_async_copy(mine, mine, other_sem.at[tile]).wait()
        chip_ref[tile] = local_ref[tile] * decay_ref[POWERS.index(tokens), tile] + other_ref[tile]
        for half in range(parties):
            owner = owner_of(half, tile)
            piece = chip_ref.at[tile, half * depth : (half + 1) * depth]

            @pl.when(owner == me)
            def _():
                pltpu.make_async_copy(piece, pieces_ref.at[chip], piece_sem.at[chip // 4]).start()

            @pl.when(owner != me)
            def _():
                pltpu.make_async_remote_copy(
                    src_ref=piece,
                    dst_ref=pieces_ref.at[chip],
                    send_sem=send_sem,
                    recv_sem=piece_sem.at[chip // 4],
                    device_id={"seq": owner},
                    device_id_type=MESH,
                ).start()

        return carry

    def quiet_block(n, carry):
        wait_pair(n)
        gather_rows(n - 1)
        run_block(n)
        return carry

    def sending_block(n, carry):
        quiet_block(n, carry)
        send_local(n - 1)

        @pl.when(core == 0)
        def _():
            send_piece(n - QUIET, 0)

        return carry

    def send_earlier(n, carry):
        send_local(n)
        return carry

    late_loads = [
        load(src, dst, load_sem.at[n + 1])
        for n, (src, dst) in enumerate(
            ((res_hbm, res_ref), (q_hbm, q_ref), (skip_hbm, skip_ref), (gain_hbm, gain_ref))
        )
    ]
    for copy in late_loads:
        copy.start()
    wait_pair(0)
    run_block(0)
    lax.fori_loop(1, QUIET, quiet_block, 0)
    sends = parties * tiles - jnp.where(is_owner, 1, 0)
    pl.semaphore_wait(barrier, chans - 1 + jnp.where(core == 0, sends, 1))
    lax.fori_loop(0, QUIET - 1, send_earlier, 0)
    lax.fori_loop(QUIET, tiles, sending_block, 0)
    gather_rows(tiles - 1)
    send_local(tiles - 1)

    @pl.when(core == 0)
    def _():
        lax.fori_loop(tiles - QUIET, tiles, send_piece, 0)
        pltpu.make_async_remote_copy(
            src_ref=local_ref,
            dst_ref=other_ref,
            send_sem=pair_sem,
            recv_sem=other_sem.at[0],
            device_id={"seq": me + 1},
            device_id_type=MESH,
        ).start()

    for copy in late_loads:
        copy.wait()
    for power in (32, 64, 128):
        set_decay(power)

    def local_part(tile, carry):
        cols = lanes_of(tile)
        q32_ref[tile] = q_ref[:, cols].astype(F32)
        g_ref[...] = k_ref[:, cols].astype(F32) * v_ref[:, cols].astype(F32)
        decay = [decay_row(1, tile, m) for m in range(modes)]
        stride = [decay_row(4, tile, m) for m in range(modes)]
        held = None
        for i in range(0, sub, 4):
            g = [g_ref[pl.ds(i + j, SUB, stride=sub), :] for j in range(4)]
            for j in range(4):
                sorted_ref[(i + j) * SUB : (i + j + 1) * SUB, :] = g[j]
            step = [((g[0] * a + g[1]) * a + g[2]) * a + g[3] for a in decay]
            held = step if held is None else [h * a + t for h, a, t in zip(held, stride, step)]
        for m in range(modes):
            rate = row(rate_ref, m, cols) * (-1.0 / length)
            lead_ref[tile, m] = row(res_ref, m, cols) * jnp.exp(rate * (rows_f + 1.0))
            for n in (1, 2, 4):
                held[m] = held[m] + decay_row(n * sub, tile, m) * shift_rows(held[m], n, rows)
            held[m] = shift_rows(held[m], 1, rows)
        weight = [row(res_ref, m, cols) for m in range(modes)]
        skip = row(skip_ref, 0, cols)
        for i in range(sub):
            spots = pl.ds(i, SUB, stride=sub)
            g = sorted_ref[i * SUB : (i + 1) * SUB, :]
            held = [h * a + g for h, a in zip(held, decay)]
            terms = [h * w for h, w in zip(held, weight)] + [skip * g]
            while len(terms) > 1:
                terms = [sum(terms[n : n + 2]) for n in range(0, len(terms), 2)]
            y_ref[tile, spots, :] = terms[0]
        return carry

    lax.fori_loop(0, tiles, local_part, 0)
    square_ref[...] = jnp.zeros_like(square_ref)

    @pl.when(is_owner)
    def _():
        mine = pl.ds(pl.multiple_of(which * depth, depth), depth)
        whole = jnp.exp(rate_ref[mine, lanes_of(own_tile)] * (-2.0 * tokens / length))

        def send_back(p, to):
            @pl.when(to == me)
            def _():
                pltpu.make_async_copy(
                    prefix_ref.at[p], state_ref.at[own_tile, mine], state_sem.at[own_tile]
                ).start()

            @pl.when(to != me)
            def _():
                pltpu.make_async_remote_copy(
                    src_ref=prefix_ref.at[p],
                    dst_ref=state_ref.at[own_tile, mine],
                    send_sem=back_sem,
                    recv_sem=state_sem.at[own_tile],
                    device_id={"seq": to},
                    device_id_type=MESH,
                ).start()

        def give(p):
            send_back(p, 2 * p)

            @pl.when(lax.rem(p, 8) < DIRECT_Z)
            def _():
                send_back(p, 2 * p + 1)

        def take_group(n, total, at_once):
            for j in range(4):
                p = n * 4 + j
                prefix_ref[p] = total
                if at_once:
                    give(p)
                total = total * whole + pieces_ref[p]
            return total

        def give_group(n):
            for j in range(4):
                give(n * 4 + j)

        def await_group(n):
            some = pieces_ref.at[pl.ds(n * 4, 4)]
            pltpu.make_async_copy(some, some, piece_sem.at[n]).wait()

        for line in range(groups // 2):
            await_group(2 * line)

        def one_line(line, total):
            @pl.when(line == 1)
            def _():
                give_group(2 * line - 1)

            total = take_group(2 * line, total, True)

            @pl.when(line > 1)
            def _():
                give_group(2 * line - 1)

            await_group(2 * line + 1)
            return take_group(2 * line + 1, total, False)

        lax.fori_loop(0, groups // 2, one_line, jnp.zeros((depth, LANES), F32))
        give_group(groups - 1)

    @pl.when(core == 1)
    def _():
        pltpu.make_async_copy(other_ref, other_ref, other_sem.at[0]).wait()

    def add_state(n, carry):
        tile = near_first(n)
        cols = lanes_of(tile)
        arrived = state_ref.at[tile]
        pltpu.make_async_copy(arrived, arrived, state_sem.at[tile]).wait()

        @pl.when((core == 0) & jnp.logical_not(direct))
        def _():
            pltpu.make_async_remote_copy(
                src_ref=state_ref.at[tile],
                dst_ref=state_ref.at[tile],
                send_sem=pair_sem,
                recv_sem=state_sem.at[tile],
                device_id={"seq": me + 1},
                device_id_type=MESH,
            ).start()

        state = state_ref[tile]
        start_ref[...] = jnp.where(core == 1, state * decay_ref[POWERS.index(tokens), tile] + other_ref[tile], state)
        gain = row(gain_ref, 0, cols)
        eighth = [decay_row(SUB, tile, m) for m in range(modes)]
        terms = [
            lead_ref[tile, m] * jnp.broadcast_to(start_ref[m : m + 1], (SUB, LANES))
            for m in range(modes)
        ]
        for i in range(steps):
            spots = pl.ds(i * SUB, SUB)
            total = list(terms)
            while len(total) > 1:
                total = [total[n] + total[n + 1] for n in range(0, len(total), 2)]
            mixed = q32_ref[tile, spots, :] * (y_ref[tile, spots, :] + total[0])
            y_ref[tile, spots, :] = mixed * gain
            square_ref[spots, :] += mixed * mixed
            if i + 1 < steps:
                terms = [t * a for t, a in zip(terms, eighth)]
        return carry

    lax.fori_loop(0, tiles, add_state, 0)

    lanes = lax.broadcasted_iota(jnp.int32, (SUB, LANES), 1)
    part = jnp.zeros((SUB, LANES), F32)
    for i in range(steps):
        sums = jnp.sum(square_ref[i * SUB : (i + 1) * SUB, :], axis=1, keepdims=True)
        part = jnp.where(lanes == i, sums, part)
    part_ref[...] = part
    for n in (2, 1, 3):
        pltpu.make_async_remote_copy(
            src_ref=part_ref,
            dst_ref=parts_ref.at[n - 1],
            send_sem=part_send,
            recv_sem=part_sem,
            device_id={"chan": lax.rem(chan + n, chans)},
            device_id_type=MESH,
        ).start()
    pltpu.make_async_copy(parts_ref, parts_ref, part_sem).wait()
    whole_sum = part
    for n in range(1, chans):
        whole_sum = whole_sum + parts_ref[n - 1]
    scale = lax.rsqrt(whole_sum * (1.0 / (channels * chans)) + 1e-06)
    for i in range(0, steps, 2):
        above = jnp.broadcast_to(scale[:, i : i + 1], (SUB, LANES))
        below = jnp.broadcast_to(scale[:, i + 1 : i + 2], (SUB, LANES))
        both = jnp.concatenate([above, below], axis=0)
        spots = slice(i * SUB, (i + 2) * SUB)
        for tile in range(tiles):
            cols = slice(tile * LANES, (tile + 1) * LANES)
            out_ref[spots, cols] = (y_ref[tile, spots, :] * both).astype(out_ref.dtype)

    pltpu.make_async_copy(parts_ref, parts_ref, part_send).wait()

    pltpu.make_async_copy(local_ref, local_ref, pair_sem).wait()

    @pl.when((core == 0) & jnp.logical_not(direct))
    def _():
        pltpu.make_async_copy(state_ref, state_ref, pair_sem).wait()

    def sent(count, sem):
        some = prefix_ref.at[pl.ds(0, count)]
        pltpu.make_async_copy(some, some, sem).wait()

    @pl.when((core == 0) & is_owner)
    def _():
        sent(parties * tiles - 1, send_sem)

    @pl.when((core == 0) & jnp.logical_not(is_owner))
    def _():
        sent(parties * tiles, send_sem)

    @pl.when(is_owner)
    def _():
        sent(chips - 1, back_sem)
        sent(4 * DIRECT_Z, back_sem)


def per_device(devices, chans, q, k, v, residues, rates, skip, gain):
    tokens, channels = q.shape
    modes = residues.shape[1]
    tiles = channels // LANES
    chips = devices // 2
    bf16 = q.dtype
    inputs = (q, k, v, residues.T, rates.T, skip[None, :], gain[None, :])
    vmem = pltpu.VMEM
    dma = pltpu.SemaphoreType.DMA
    whole = vmem((tokens, channels), bf16)
    table = vmem((modes, channels), F32)
    line = vmem((1, channels), F32)
    by_tile = vmem((tiles, tokens, LANES), F32)
    by_mode = vmem((tiles, modes, SUB, LANES), F32)
    by_token = vmem((tokens, LANES), F32)
    by_chip = vmem((chips, modes // len(OWNER_Z), LANES), F32)
    packed = vmem((tiles, modes, LANES), F32)
    return pl.pallas_call(
        functools.partial(body, float(tokens * devices)),
        out_shape=jax.ShapeDtypeStruct((tokens, channels), bf16),
        in_specs=[pl.BlockSpec(memory_space=pltpu.HBM)] * len(inputs),
        out_specs=pl.BlockSpec(memory_space=vmem),
        scratch_shapes=[whole, whole, whole, table, table, line, line]
        + [vmem((len(POWERS), tiles, modes, LANES), F32)]
        + [by_token, by_token, by_tile, by_tile, by_mode, by_mode]
        + [packed, packed, packed, packed, vmem((modes, LANES), F32), by_token]
        + [by_chip, by_chip]
        + [vmem((SUB, LANES), F32), vmem((chans - 1, SUB, LANES), F32)]
        + [dma((5,)), dma((tiles // 2,)), dma((tiles // 2,)), dma((tiles,)), dma, dma]
        + [dma((chips // 4,)), dma, dma((tiles,)), dma, dma],
        compiler_params=pltpu.CompilerParams(
            collective_id=0, has_side_effects=True, vmem_limit_bytes=24 * 1024 * 1024
        ),
    )(*[pltpu.with_memory_space_constraint(a, pltpu.HBM) for a in inputs])


def solution(mesh):
    devices, chans = mesh.shape["seq"], mesh.shape["chan"]
    return jax.shard_map(
        functools.partial(per_device, devices, chans),
        mesh=mesh,
        in_specs=(
            P("seq", "chan"),
            P("seq", "chan"),
            P("seq", "chan"),
            P("chan", None),
            P("chan", None),
            P("chan"),
            P("chan"),
        ),
        out_specs=P("seq", "chan"),
        check_vma=False,
    )
```

```python
import functools

import jax
import jax.numpy as jnp
from jax import lax
from jax.experimental import pallas as pl
from jax.experimental.pallas import tpu as pltpu
from jax.sharding import PartitionSpec as P

MESH = pl.DeviceIdType.MESH
F32 = jnp.float32
LANES = 128
SUB = 8
OWNER_Z = (0, 1)
DIRECT_Z = 3
QUIET = 4
POWERS = (1, 2, 4, 8, 16, 32, 64, 128, 256)


def shift_rows(x, n, rows):
    return jnp.where(rows >= n, pltpu.roll(x, n, 0), 0.0)


def body(
    length,
    q_hbm,
    k_hbm,
    v_hbm,
    res_hbm,
    rate_hbm,
    skip_hbm,
    gain_hbm,
    y_ref,
    scale_ref,
    q_ref,
    k_ref,
    v_ref,
    res_ref,
    rate_ref,
    skip_ref,
    gain_ref,
    decay_ref,
    g_ref,
    sorted_ref,
    q32_ref,
    ends_ref,
    lead_ref,
    local_ref,
    other_ref,
    chip_ref,
    state_ref,
    start_ref,
    square_ref,
    pieces_ref,
    prefix_ref,
    part_ref,
    parts_ref,
    load_sem,
    key_sem,
    value_sem,
    other_sem,
    pair_sem,
    send_sem,
    piece_sem,
    back_sem,
    state_sem,
    part_send,
    part_sem,
):
    me = lax.axis_index("seq")
    chan = lax.axis_index("chan")
    tokens, channels = q_ref.shape
    modes = res_ref.shape[0]
    tiles = channels // LANES
    steps = tokens // SUB
    sub = tokens // SUB
    chips = pieces_ref.shape[0]
    groups = chips // 4
    chans = parts_ref.shape[0] + 1
    chip = me // 2
    x, z, core = me // 16, lax.rem(chip, 8), lax.rem(me, 2)
    parties = len(OWNER_Z)
    is_owner = (z == OWNER_Z[0]) | (z == OWNER_Z[-1])
    which = jnp.where(z == OWNER_Z[0], 0, parties - 1)
    own_tile = 2 * x + core
    depth = modes // parties
    direct = z < DIRECT_Z

    def owner_of(half, tile):
        return ((tile // 2) * 8 + OWNER_Z[half]) * 2 + lax.rem(tile, 2)

    def far_first(n):
        pair = n // 2
        turn = jnp.where(pair == 0, 2, jnp.where(pair == 1, 3, jnp.where(pair == 2, 1, 0)))
        return lax.rem(x + turn, 4) * 2 + lax.rem(n, 2)

    def near_first(n):
        pair = n // 2
        turn = jnp.where(pair == 1, 3, jnp.where(pair == 2, 1, jnp.where(pair == 3, 2, 0)))
        return lax.rem(x + turn, 4) * 2 + lax.rem(n, 2)

    def lanes_of(tile, width=1):
        return pl.ds(pl.multiple_of(tile * LANES, LANES), width * LANES)

    def load(src, dst, sem):
        return pltpu.make_async_copy(src, dst, sem)

    def load_pair(pair):
        cols = lanes_of(far_first(2 * pair), 2)
        return (
            load(k_hbm.at[:, cols], k_ref.at[:, cols], key_sem.at[pair]),
            load(v_hbm.at[:, cols], v_ref.at[:, cols], value_sem.at[pair]),
        )

    rate_load = load(rate_hbm, rate_ref, load_sem.at[0])
    rate_load.start()
    for pair in range(tiles // 2):
        for copy in load_pair(pair):
            copy.start()

    barrier = pltpu.get_barrier_semaphore()

    @pl.when(is_owner)
    def _():
        def greet(n, carry):
            sender = lax.rem(chip + n, chips)

            @pl.when(2 * sender != me)
            def _():
                pl.semaphore_signal(
                    barrier, inc=1, device_id={"seq": 2 * sender}, device_id_type=MESH
                )

            return carry

        lax.fori_loop(0, chips, greet, 0)

    @pl.when(core == 0)
    def _():
        pl.semaphore_signal(barrier, inc=1, device_id={"seq": me + 1}, device_id_type=MESH)

    for n in range(1, chans):
        pl.semaphore_signal(
            barrier, inc=1, device_id={"chan": lax.rem(chan + n, chans)}, device_id_type=MESH
        )

    rows = lax.broadcasted_iota(jnp.int32, (SUB, LANES), 0)
    rows_f = rows.astype(F32)

    def set_decay(power):
        for tile in range(tiles):
            rate = rate_ref[:, tile * LANES : (tile + 1) * LANES]
            decay_ref[POWERS.index(power), tile] = jnp.exp(rate * (-float(power) / length))

    rate_load.wait()
    for power in (1, 2, 4, 8, 16, tokens):
        set_decay(power)

    def row(ref, m, cols):
        return jnp.broadcast_to(ref[m : m + 1, cols], (SUB, LANES))

    def decay_row(power, tile, m):
        return jnp.broadcast_to(decay_ref[POWERS.index(power), tile, m : m + 1], (SUB, LANES))


    def wait_pair(n):
        @pl.when(lax.rem(n, 2) == 0)
        def _():
            for copy in load_pair(n // 2):
                copy.wait()

    def run_block(n):
        tile = far_first(n)
        cols = lanes_of(tile)
        eighth = [decay_row(8, tile, m) for m in range(modes)]
        stride = [decay_row(16, tile, m) for m in range(modes)]
        held = None
        for i in range(0, tokens, 2 * SUB):
            spots = slice(i, i + 2 * SUB)
            g = k_ref[spots, cols].astype(F32) * v_ref[spots, cols].astype(F32)
            step = [g[:SUB] * a + g[SUB:] for a in eighth]
            held = step if held is None else [h * a + t for h, a, t in zip(held, stride, step)]
        for m in range(modes):
            ends_ref[tile, m] = held[m]

    def gather_rows(n):
        tile = far_first(n)
        for m in range(modes):
            end = ends_ref[tile, m]
            for power in (1, 2, 4):
                end = end + decay_row(power, tile, m) * pltpu.roll(end, power, 0)
            local_ref[tile, m : m + 1] = end[SUB - 1 :]

    def send_local(n):
        tile = far_first(n)

        @pl.when(core == 1)
        def _():
            pltpu.make_async_remote_copy(
                src_ref=local_ref.at[tile],
                dst_ref=other_ref.at[tile],
                send_sem=pair_sem,
                recv_sem=other_sem.at[tile],
                device_id={"seq": me - 1},
                device_id_type=MESH,
            ).start()

    def send_piece(n, carry):
        tile = far_first(n)
        mine = other_ref.at[tile]
        pltpu.make_async_copy(mine, mine, other_sem.at[tile]).wait()
        chip_ref[tile] = local_ref[tile] * decay_ref[POWERS.index(tokens), tile] + other_ref[tile]
        for half in range(parties):
            owner = owner_of(half, tile)
            piece = chip_ref.at[tile, half * depth : (half + 1) * depth]

            @pl.when(owner == me)
            def _():
                pltpu.make_async_copy(piece, pieces_ref.at[chip], piece_sem.at[chip // 4]).start()

            @pl.when(owner != me)
            def _():
                pltpu.make_async_remote_copy(
                    src_ref=piece,
                    dst_ref=pieces_ref.at[chip],
                    send_sem=send_sem,
                    recv_sem=piece_sem.at[chip // 4],
                    device_id={"seq": owner},
                    device_id_type=MESH,
                ).start()

        return carry

    def quiet_block(n, carry):
        wait_pair(n)
        gather_rows(n - 1)
        run_block(n)
        return carry

    def sending_block(n, carry):
        quiet_block(n, carry)
        send_local(n - 1)

        @pl.when(core == 0)
        def _():
            send_piece(n - QUIET, 0)

        return carry

    def send_earlier(n, carry):
        send_local(n)
        return carry

    late_loads = [
        load(src, dst, load_sem.at[n + 1])
        for n, (src, dst) in enumerate(
            ((res_hbm, res_ref), (q_hbm, q_ref), (skip_hbm, skip_ref), (gain_hbm, gain_ref))
        )
    ]
    for copy in late_loads:
        copy.start()
    wait_pair(0)
    run_block(0)
    lax.fori_loop(1, QUIET, quiet_block, 0)
    sends = parties * tiles - jnp.where(is_owner, 1, 0)
    pl.semaphore_wait(barrier, chans - 1 + jnp.where(core == 0, sends, 1))
    lax.fori_loop(0, QUIET - 1, send_earlier, 0)
    lax.fori_loop(QUIET, tiles, sending_block, 0)
    gather_rows(tiles - 1)
    send_local(tiles - 1)

    @pl.when(core == 0)
    def _():
        lax.fori_loop(tiles - QUIET, tiles, send_piece, 0)
        pltpu.make_async_remote_copy(
            src_ref=local_ref,
            dst_ref=other_ref,
            send_sem=pair_sem,
            recv_sem=other_sem.at[0],
            device_id={"seq": me + 1},
            device_id_type=MESH,
        ).start()

    for copy in late_loads:
        copy.wait()
    for power in (32, 64, 128):
        set_decay(power)

    def local_part(tile, carry):
        cols = lanes_of(tile)
        q32_ref[tile] = q_ref[:, cols].astype(F32)
        g_ref[...] = k_ref[:, cols].astype(F32) * v_ref[:, cols].astype(F32)
        decay = [decay_row(1, tile, m) for m in range(modes)]
        stride = [decay_row(4, tile, m) for m in range(modes)]
        held = None
        for i in range(0, sub, 4):
            g = [g_ref[pl.ds(i + j, SUB, stride=sub), :] for j in range(4)]
            for j in range(4):
                sorted_ref[(i + j) * SUB : (i + j + 1) * SUB, :] = g[j]
            step = [((g[0] * a + g[1]) * a + g[2]) * a + g[3] for a in decay]
            held = step if held is None else [h * a + t for h, a, t in zip(held, stride, step)]
        for m in range(modes):
            rate = row(rate_ref, m, cols) * (-1.0 / length)
            lead_ref[tile, m] = row(res_ref, m, cols) * jnp.exp(rate * (rows_f + 1.0))
            for n in (1, 2, 4):
                held[m] = held[m] + decay_row(n * sub, tile, m) * shift_rows(held[m], n, rows)
            held[m] = shift_rows(held[m], 1, rows)
        weight = [row(res_ref, m, cols) for m in range(modes)]
        skip = row(skip_ref, 0, cols)
        for i in range(sub):
            spots = pl.ds(i, SUB, stride=sub)
            g = sorted_ref[i * SUB : (i + 1) * SUB, :]
            held = [h * a + g for h, a in zip(held, decay)]
            terms = [h * w for h, w in zip(held, weight)] + [skip * g]
            while len(terms) > 1:
                terms = [sum(terms[n : n + 2]) for n in range(0, len(terms), 2)]
            y_ref[tile, spots, :] = terms[0]
        return carry

    lax.fori_loop(0, tiles, local_part, 0)
    square_ref[...] = jnp.zeros_like(square_ref)

    @pl.when(is_owner)
    def _():
        mine = pl.ds(pl.multiple_of(which * depth, depth), depth)
        whole = jnp.exp(rate_ref[mine, lanes_of(own_tile)] * (-2.0 * tokens / length))

        def send_back(p, to):
            @pl.when(to == me)
            def _():
                pltpu.make_async_copy(
                    prefix_ref.at[p], state_ref.at[own_tile, mine], state_sem.at[own_tile]
                ).start()

            @pl.when(to != me)
            def _():
                pltpu.make_async_remote_copy(
                    src_ref=prefix_ref.at[p],
                    dst_ref=state_ref.at[own_tile, mine],
                    send_sem=back_sem,
                    recv_sem=state_sem.at[own_tile],
                    device_id={"seq": to},
                    device_id_type=MESH,
                ).start()

        def give(p):
            send_back(p, 2 * p)

            @pl.when(lax.rem(p, 8) < DIRECT_Z)
            def _():
                send_back(p, 2 * p + 1)

        def take_group(n, total, at_once):
            for j in range(4):
                p = n * 4 + j
                prefix_ref[p] = total
                if at_once:
                    give(p)
                total = total * whole + pieces_ref[p]
            return total

        def give_group(n):
            for j in range(4):
                give(n * 4 + j)

        def await_group(n):
            some = pieces_ref.at[pl.ds(n * 4, 4)]
            pltpu.make_async_copy(some, some, piece_sem.at[n]).wait()

        for line in range(groups // 2):
            await_group(2 * line)

        def one_line(line, total):
            @pl.when(line == 1)
            def _():
                give_group(2 * line - 1)

            total = take_group(2 * line, total, True)

            @pl.when(line > 1)
            def _():
                give_group(2 * line - 1)

            await_group(2 * line + 1)
            return take_group(2 * line + 1, total, False)

        lax.fori_loop(0, groups // 2, one_line, jnp.zeros((depth, LANES), F32))
        give_group(groups - 1)

    @pl.when(core == 1)
    def _():
        pltpu.make_async_copy(other_ref, other_ref, other_sem.at[0]).wait()

    def add_state(n, carry):
        tile = near_first(n)
        cols = lanes_of(tile)
        arrived = state_ref.at[tile]
        pltpu.make_async_copy(arrived, arrived, state_sem.at[tile]).wait()

        @pl.when((core == 0) & jnp.logical_not(direct))
        def _():
            pltpu.make_async_remote_copy(
                src_ref=state_ref.at[tile],
                dst_ref=state_ref.at[tile],
                send_sem=pair_sem,
                recv_sem=state_sem.at[tile],
                device_id={"seq": me + 1},
                device_id_type=MESH,
            ).start()

        state = state_ref[tile]
        start_ref[...] = jnp.where(core == 1, state * decay_ref[POWERS.index(tokens), tile] + other_ref[tile], state)
        gain = row(gain_ref, 0, cols)
        eighth = [decay_row(SUB, tile, m) for m in range(modes)]
        terms = [
            lead_ref[tile, m] * jnp.broadcast_to(start_ref[m : m + 1], (SUB, LANES))
            for m in range(modes)
        ]
        for i in range(steps):
            spots = pl.ds(i * SUB, SUB)
            total = list(terms)
            while len(total) > 1:
                total = [total[n] + total[n + 1] for n in range(0, len(total), 2)]
            mixed = q32_ref[tile, spots, :] * (y_ref[tile, spots, :] + total[0])
            y_ref[tile, spots, :] = mixed * gain
            square_ref[spots, :] += mixed * mixed
            if i + 1 < steps:
                terms = [t * a for t, a in zip(terms, eighth)]
        return carry

    lax.fori_loop(0, tiles, add_state, 0)

    lanes = lax.broadcasted_iota(jnp.int32, (SUB, LANES), 1)
    part = jnp.zeros((SUB, LANES), F32)
    for i in range(steps):
        sums = jnp.sum(square_ref[i * SUB : (i + 1) * SUB, :], axis=1, keepdims=True)
        part = jnp.where(lanes == i, sums, part)
    part_ref[...] = part
    for n in (2, 1, 3):
        pltpu.make_async_remote_copy(
            src_ref=part_ref,
            dst_ref=parts_ref.at[n - 1],
            send_sem=part_send,
            recv_sem=part_sem,
            device_id={"chan": lax.rem(chan + n, chans)},
            device_id_type=MESH,
        ).start()
    pltpu.make_async_copy(parts_ref, parts_ref, part_sem).wait()
    whole_sum = part
    for n in range(1, chans):
        whole_sum = whole_sum + parts_ref[n - 1]
    scale = lax.rsqrt(whole_sum * (1.0 / (channels * chans)) + 1e-06)
    scale_ref[...] = scale

    pltpu.make_async_copy(parts_ref, parts_ref, part_send).wait()

    pltpu.make_async_copy(local_ref, local_ref, pair_sem).wait()

    @pl.when((core == 0) & jnp.logical_not(direct))
    def _():
        pltpu.make_async_copy(state_ref, state_ref, pair_sem).wait()

    def sent(count, sem):
        some = prefix_ref.at[pl.ds(0, count)]
        pltpu.make_async_copy(some, some, sem).wait()

    @pl.when((core == 0) & is_owner)
    def _():
        sent(parties * tiles - 1, send_sem)

    @pl.when((core == 0) & jnp.logical_not(is_owner))
    def _():
        sent(parties * tiles, send_sem)

    @pl.when(is_owner)
    def _():
        sent(chips - 1, back_sem)
        sent(4 * DIRECT_Z, back_sem)


def finish(y_ref, scale_ref, out_hbm, out_ref, sems):
    tiles, tokens, _ = y_ref.shape
    chunk = tokens // sems.shape[0]
    scale = scale_ref[...]
    copies = []
    for n in range(sems.shape[0]):
        for i in range(n * chunk, (n + 1) * chunk, 2 * SUB):
            lane = i // SUB
            above = jnp.broadcast_to(scale[:, lane : lane + 1], (SUB, LANES))
            below = jnp.broadcast_to(scale[:, lane + 1 : lane + 2], (SUB, LANES))
            both = jnp.concatenate([above, below], axis=0)
            spots = slice(i, i + 2 * SUB)
            for tile in range(tiles):
                cols = slice(tile * LANES, (tile + 1) * LANES)
                out_ref[spots, cols] = (y_ref[tile, spots, :] * both).astype(out_ref.dtype)
        part = pl.ds(n * chunk, chunk)
        copies.append(pltpu.make_async_copy(out_ref.at[part], out_hbm.at[part], sems.at[n]))
        copies[-1].start()
    for copy in copies:
        copy.wait()


def per_device(devices, chans, q, k, v, residues, rates, skip, gain):
    tokens, channels = q.shape
    modes = residues.shape[1]
    tiles = channels // LANES
    chips = devices // 2
    bf16 = q.dtype
    inputs = (q, k, v, residues.T, rates.T, skip[None, :], gain[None, :])
    vmem = pltpu.VMEM
    dma = pltpu.SemaphoreType.DMA
    whole = vmem((tokens, channels), bf16)
    table = vmem((modes, channels), F32)
    line = vmem((1, channels), F32)
    by_tile = vmem((tiles, tokens, LANES), F32)
    by_mode = vmem((tiles, modes, SUB, LANES), F32)
    by_token = vmem((tokens, LANES), F32)
    by_chip = vmem((chips, modes // len(OWNER_Z), LANES), F32)
    packed = vmem((tiles, modes, LANES), F32)
    y, scale = pl.pallas_call(
        functools.partial(body, float(tokens * devices)),
        out_shape=[
            jax.ShapeDtypeStruct((tiles, tokens, LANES), F32),
            jax.ShapeDtypeStruct((SUB, LANES), F32),
        ],
        in_specs=[pl.BlockSpec(memory_space=pltpu.HBM)] * len(inputs),
        out_specs=[pl.BlockSpec(memory_space=vmem)] * 2,
        scratch_shapes=[whole, whole, whole, table, table, line, line]
        + [vmem((len(POWERS), tiles, modes, LANES), F32)]
        + [by_token, by_token, by_tile, by_mode, by_mode]
        + [packed, packed, packed, packed, vmem((modes, LANES), F32), by_token]
        + [by_chip, by_chip]
        + [vmem((SUB, LANES), F32), vmem((chans - 1, SUB, LANES), F32)]
        + [dma((5,)), dma((tiles // 2,)), dma((tiles // 2,)), dma((tiles,)), dma, dma]
        + [dma((chips // 4,)), dma, dma((tiles,)), dma, dma],
        compiler_params=pltpu.CompilerParams(
            collective_id=0, has_side_effects=True, vmem_limit_bytes=24 * 1024 * 1024
        ),
    )(*[pltpu.with_memory_space_constraint(a, pltpu.HBM) for a in inputs])
    return pl.pallas_call(
        finish,
        out_shape=jax.ShapeDtypeStruct((tokens, channels), bf16),
        in_specs=[pl.BlockSpec(memory_space=vmem)] * 2,
        out_specs=pl.BlockSpec(memory_space=pltpu.HBM),
        scratch_shapes=[whole, dma((4,))],
        compiler_params=pltpu.CompilerParams(vmem_limit_bytes=16 * 1024 * 1024),
    )(*[pltpu.with_memory_space_constraint(a, pltpu.VMEM) for a in (y, scale)])


def solution(mesh):
    devices, chans = mesh.shape["seq"], mesh.shape["chan"]
    return jax.shard_map(
        functools.partial(per_device, devices, chans),
        mesh=mesh,
        in_specs=(
            P("seq", "chan"),
            P("seq", "chan"),
            P("seq", "chan"),
            P("chan", None),
            P("chan", None),
            P("chan"),
            P("chan"),
        ),
        out_specs=P("seq", "chan"),
        check_vma=False,
    )
```
